128 devices in a mesh: table: 8 (over y, core), replica: 16 (over z, x).
Axes of the slice: x: 4, y: 4, z: 4, core: 2. Of those that a mesh axis runs over, the one named last changes fastest.
Arguments:
- hot_ids: int32 [16384, 8], P(('table', 'replica')), may hold values from 0 to 4095
- cold_owner: int32 [16384, 8], P(('table', 'replica')), may hold values from 0 to 127, all different within a row; in each aligned block of 128 rows (0 to 127, 128 to 255, ...) at most 16 rows name the same one
- cold_row: int32 [16384, 8], P(('table', 'replica')), may hold values from 0 to 2047
- cold_exp: int32 [16384, 8], P(('table', 'replica')), may hold values from 0 to 2
- labels: float32 [16384], P(('table', 'replica')), may hold values from 0 to 1
- head_w: float32 [4096], replicated, may hold values from -0.3 to 0.3
- hot_table: float32 [4096, 256], P('table'), may hold values from -2 to 2
- hot_acc: float32 [4096, 256], P('table'), may hold values from 0.01 to 1
- cold_table: float32 [262144, 256], P(('table', 'replica')), may hold values from -2 to 2
- cold_acc: float32 [262144, 256], P(('table', 'replica')), may hold values from 1e-06 to 0.0001
- tower_w: float32 [512, 4096], P(None, 'table'), may hold values from -0.25 to 0.25
- tower_acc: float32 [512, 4096], P(None, 'table'), may hold values from 1 to 100
Outputs:
- new_hot_table: float32 [4096, 256], P('table')
- new_hot_acc: float32 [4096, 256], P('table')
- new_cold_table: float32 [262144, 256], P(('table', 'replica'))
- new_cold_acc: float32 [262144, 256], P(('table', 'replica'))
- new_tower_w: float32 [512, 4096], P(None, 'table')
- new_tower_acc: float32 [512, 4096], P(None, 'table')
The draws below stay inside these ranges and needn't reach their ends.
Inputs may be any that keep to these rules, and one draw needn't show every extreme that they name: `cold_owner`: the 8 owners of one sample differ; among the samples of one device no owner is named more than 16 times, a bound that some block reaches.
All inputs are finite; a program needn't handle non-finite values.
Results may differ from the reference program's by a relative error of at most 0.0035.
The reference program's roundings to bfloat16 on the way (of `features`, `dpre` and `item_grad`) count: a program that leaves them out, or rounds other values in their place, can miss the bound.
Values may be sent and summed in bfloat16 or wider, within the bound.
No kernel may reach another device: no remote copies, remote signals or barrier semaphores. Data moves between devices by JAX's collectives and lax.ppermute only.
A program may use at most 128 MiB of HBM per device.

```python
import math
import jax
import jax.numpy as jnp
import numpy as np
from jax import lax

D = 256
H = 4096
B_DEV = 128
KH = 8
KC = 8
COLD_DEV = 2048
DIN = 512
SAMPLES = 16384
HOT = 4096
COLD = 262144
CAP = 16
DEVICES = 128


def plant(result, key, smallest, top_value):
    longest = result.shape.index(max(result.shape))
    spots = []
    for shift in (0, 1):
        where = [jax.random.randint(jax.random.fold_in(key, axis), (), 0, length) for axis, length in enumerate(result.shape)]
        where[longest] = (where[longest] + shift) % result.shape[longest]
        spots.append(tuple(where))
    return result.at[spots[0]].set(smallest).at[spots[1]].set(top_value)


def block_levels(rng, extent, cuts, low, largest):
    loudness = 1.0
    for axis_at, blocks in cuts:
        draws = jax.random.uniform(jax.random.fold_in(jax.random.fold_in(rng, 6), axis_at), (blocks,), jnp.float32, low / len(cuts), largest / len(cuts))
        loudness = loudness * jnp.repeat(jnp.exp(draws), extent[axis_at] // blocks).reshape((-1,) + (1,) * (len(extent) - 1 - axis_at))
    return loudness


def cumulative_ranks(count, lean):
    weights = [(1 << 20) // math.isqrt(rank ** lean) + 1 for rank in range(1, count + 1)]
    scale = 1 + sum(weights) // (1 << 30)
    return np.cumsum(np.array([max(1, weight // scale) for weight in weights]))


def ranked(rng, shape, number_of, lean):
    table = cumulative_ranks(number_of, lean)
    ticket = jax.random.randint(jax.random.fold_in(rng, 1), shape, 0, int(table[number_of - 1]))
    grade = jnp.searchsorted(jnp.asarray(table, jnp.int32), ticket, side="right")
    return jax.random.permutation(jax.random.fold_in(rng, 2), number_of)[grade].astype(jnp.int32)


def routed_block(own_key, own, number, rows, number_of, top, limit, skew):
    ranking = jax.random.permutation(own_key, number_of)
    heavy_load, ordinary = shares(number_of, rows * top, limit, skew, True), shares(number_of, rows * top, limit, skew, False)
    places = jnp.arange(number_of)

    def named(lengths, offset_by):
        used = int((lengths > 0).sum())
        fixed = max(1, used // 4)
        moved = fixed + (places - fixed + offset_by * (used - fixed)) % max(1, number_of - fixed)
        return jnp.zeros((number_of,), jnp.int32).at[ranking[jnp.where(places < fixed, places, moved)]].set(jnp.asarray(lengths, jnp.int32))

    lengths = jnp.where(number % 4 == 0, named(heavy_load, number // 4), named(ordinary, number - number // 4 - 1))
    mixed = jax.random.permutation(jax.random.fold_in(own, 3), number_of)
    donor, taker = mixed[0:number_of // 2 * 2:2], mixed[1:number_of // 2 * 2:2]
    margin = jnp.minimum(lengths[donor] - 1, limit - lengths[taker]) // 2
    margin = jnp.where((donor == ranking[0]) | (taker == ranking[0]) | (lengths[taker] == 0), 0, jnp.maximum(margin, 0))
    moved = jax.random.randint(jax.random.fold_in(own, 4), (number_of // 2,), 0, 1 << 20) % (margin + 1)
    lengths = lengths.at[donor].add(-moved).at[taker].add(moved)
    members = jnp.searchsorted(jnp.cumsum(lengths), jnp.arange(rows * top), side="right").astype(jnp.int32)
    listing = members.reshape(top, rows).T
    listing = listing[jax.random.permutation(jax.random.fold_in(own, 1), rows)]
    offset_by = jax.random.randint(jax.random.fold_in(own, 2), (rows, 1), 0, top)
    return jnp.take_along_axis(listing, (jnp.arange(top)[None, :] + offset_by) % top, axis=1)


def shares(number_of, total, limit, lean, full):
    weights = [(1 << 20) // math.isqrt(grade ** lean) + 1 for grade in range(1, number_of + 1)]
    largest = limit if full else min(limit, max(-(-total // number_of), total * weights[0] // sum(weights)))
    least = 1 if total - largest >= number_of - 1 else 0
    counts, surplus = [largest] + [least] * (number_of - 1), total - largest - least * (number_of - 1)
    while surplus > 0:
        movable = [i for i in range(1, number_of) if counts[i] < largest] or [i for i in range(1, number_of) if counts[i] < limit]
        mass, budget = sum([weights[i] for i in movable]), surplus
        for i in movable:
            extra = min(limit - counts[i], max(1, budget * weights[i] // mass), surplus)
            counts[i] = counts[i] + extra
            surplus = surplus - extra
    return np.array(counts)


def gaussian(own_key, extent, spread, most, split=(), held_as=jnp.bfloat16):
    values = jax.random.normal(own_key, extent, jnp.float32) * spread
    if len(split) > 0:
        values = block_levels(own_key, extent, split, -0.22, 0.18) * values
    return jnp.clip(values, min=-most, max=most).astype(held_as)


def setup_inputs(seed: int = 0) -> dict:
    key_of = jax.random.split(jax.random.key(seed), 13)
    hot_ids = plant(ranked(key_of[0], (SAMPLES, KH), HOT, 1), jax.random.fold_in(key_of[0], 3), 0, HOT - 1).astype(jnp.int32)
    cold_owner_keys = jax.random.split(jax.random.fold_in(key_of[1], 1), SAMPLES // B_DEV)
    cold_owner_turns = jax.random.permutation(jax.random.fold_in(key_of[1], 3), SAMPLES // B_DEV)
    cold_owner = jax.vmap(lambda own, number: routed_block(jax.random.fold_in(key_of[1], 2), own, number, B_DEV, DEVICES, KC, CAP, 2))(cold_owner_keys, cold_owner_turns).reshape((SAMPLES, KC))
    cold_row = plant(jax.random.randint(key_of[2], (SAMPLES, KC), 0, COLD_DEV), jax.random.fold_in(key_of[2], 1), 0, COLD_DEV - 1).astype(jnp.int32)
    cold_exp = plant(jax.random.randint(key_of[3], (SAMPLES, KC), 0, 3), jax.random.fold_in(key_of[3], 1), 0, 2).astype(jnp.int32)
    labels = jnp.clip(1.0 * jax.random.uniform(key_of[4], (SAMPLES,), jnp.float32) ** block_levels(key_of[4], (SAMPLES,), ((0, 128),), -0.2, 0.2), 0.0, 1.0)
    head_w = gaussian(key_of[5], (H,), 0.05, 0.3, (), jnp.float32)
    hot_table = gaussian(key_of[6], (HOT, D), 0.3, 2.0, ((0, 8),), jnp.float32)
    hot_acc = jnp.clip(jnp.exp(math.log(1.0) - 4.6051702 * jax.random.uniform(key_of[7], (HOT, D), jnp.float32) ** block_levels(key_of[7], (HOT, D), ((0, 8),), -0.2, 0.2)), 0.01, 1.0)
    cold_table = gaussian(key_of[8], (COLD, D), 0.3, 2.0, ((0, 128),), jnp.float32)
    cold_acc = jnp.clip(jnp.exp(math.log(0.0001) - 4.6051702 * jax.random.uniform(key_of[9], (COLD, D), jnp.float32) ** block_levels(key_of[9], (COLD, D), ((0, 128),), -0.2, 0.2)), 9.999999974752427e-07, 0.0001)
    tower_w = gaussian(key_of[10], (DIN, H), DIN ** -0.5, 0.25, ((1, 8),), jnp.float32)
    tower_acc = jnp.clip(jnp.exp(math.log(100.0) - 4.6051702 * jax.random.uniform(key_of[11], (DIN, H), jnp.float32) ** block_levels(key_of[11], (DIN, H), ((1, 8),), -0.2, 0.2)), 1.0, 100.0)
    return dict(hot_ids=hot_ids, cold_owner=cold_owner, cold_row=cold_row, cold_exp=cold_exp, labels=labels, head_w=head_w, hot_table=hot_table, hot_acc=hot_acc, cold_table=cold_table, cold_acc=cold_acc, tower_w=tower_w, tower_acc=tower_acc)


learn_rate = 0.05

def adagrad(param, accum, grad):
    new_accum = accum + grad * grad
    return (param - learn_rate * grad * lax.rsqrt(new_accum), new_accum)

def reference(hot_ids, cold_owner, cold_row, cold_exp, labels, head_w, hot_table, hot_acc, cold_table, cold_acc, tower_w, tower_acc):
    hot_half = hot_table.astype(jnp.bfloat16)
    cold_half = cold_table.astype(jnp.bfloat16)
    w_half = tower_w.astype(jnp.bfloat16)
    blocks = SAMPLES // B_DEV
    inputs = (hot_ids.reshape(blocks, B_DEV, KH), cold_owner.reshape(blocks, B_DEV, KC), cold_row.reshape(blocks, B_DEV, KC), cold_exp.reshape(blocks, B_DEV, KC), labels.reshape(blocks, B_DEV))

    def step(carry, block):
        hot_grad, cold_grad, w_grad = carry
        ids_hot, owners, rowsel, expon, target = block
        global_rows = (owners * COLD_DEV + rowsel).astype(jnp.int32)
        hot_pool = lax.optimization_barrier(jnp.sum(hot_half[ids_hot].astype(jnp.float32), axis=1))
        scales = jnp.exp2(-expon.astype(jnp.float32))
        cold_pool = lax.optimization_barrier(jnp.sum(cold_half[global_rows].astype(jnp.float32) * scales[:, :, None], axis=1))
        features = jnp.concatenate([hot_pool, cold_pool], axis=1).astype(jnp.bfloat16)
        pre = jnp.dot(features, w_half, preferred_element_type=jnp.float32)
        sig = jax.nn.sigmoid(pre)
        act = pre * sig
        logit = lax.optimization_barrier(jnp.sum(act * head_w[None, :], axis=1))
        prob = jax.nn.sigmoid(logit)
        dlogit = prob - target
        dpre = (dlogit[:, None] * head_w[None, :] * sig * (1.0 + pre * (1.0 - sig))).astype(jnp.bfloat16)
        w_grad = w_grad + lax.dot_general(features, dpre, (((0,), (0,)), ((), ())), preferred_element_type=jnp.float32)
        dfeat = lax.dot_general(dpre, w_half, (((1,), (1,)), ((), ())), preferred_element_type=jnp.float32)
        dhot = dfeat[:, :D]
        dcold = dfeat[:, D:]
        hot_vals = jnp.broadcast_to(dhot[:, None, :], (B_DEV, KH, D)).reshape(-1, D)
        hot_grad = hot_grad.at[ids_hot.reshape(-1)].add(hot_vals)
        item_grad = (dcold[:, None, :] * scales[:, :, None]).astype(jnp.bfloat16)
        cold_grad = cold_grad.at[global_rows.reshape(-1)].add(item_grad.reshape(-1, D).astype(jnp.float32))
        return ((hot_grad, cold_grad, w_grad), None)
    start = (jnp.zeros((HOT, D), jnp.float32), jnp.zeros((COLD, D), jnp.float32), jnp.zeros((DIN, H), jnp.float32))
    (hot_grad, cold_grad, w_grad), _ = lax.scan(step, start, inputs)
    new_hot, new_hot_acc = adagrad(hot_table, hot_acc, hot_grad)
    new_cold, new_cold_acc = adagrad(cold_table, cold_acc, cold_grad)
    new_w, new_w_acc = adagrad(tower_w, tower_acc, w_grad)
    return (new_hot, new_hot_acc, new_cold, new_cold_acc, new_w, new_w_acc)
```

```python
import jax
import jax.numpy as jnp
from jax import lax
from jax.experimental import pallas as pl
from jax.experimental.pallas import tpu as pltpu
from jax.sharding import PartitionSpec as P

learn_rate = 0.05
bf16 = jnp.bfloat16
f32 = jnp.float32
i32 = jnp.int32
ALL = ("table", "replica")
VM = pl.BlockSpec(memory_space=pltpu.VMEM)
PARAMS = pltpu.CompilerParams(vmem_limit_bytes=48 * 1024 * 1024)


def adagrad(param, accum, grad):
    new_accum = accum + grad * grad
    return (param - learn_rate * grad * lax.rsqrt(new_accum), new_accum)


def iota(shape, axis):
    return lax.broadcasted_iota(i32, shape, axis)


def route_kernel(own_ref, row_ref, exp_ref, asks_ref, place_ref, scale_ref):
    keys, batch = own_ref.shape
    devices, capacity = asks_ref.shape
    owners = iota((devices, batch), 0)
    named = jnp.zeros((devices, batch), f32)
    rows = jnp.zeros((devices, batch), f32)
    scales = jnp.zeros((devices, batch), f32)
    expo = exp_ref[...]
    scale = jnp.where(expo == 0, 1.0, jnp.where(expo == 1, 0.5, 0.25))
    row = row_ref[...].astype(f32)
    own = own_ref[...]
    for k in range(keys):
        hit = own[k : k + 1, :] == owners
        named = jnp.where(hit, 1.0, named)
        rows = jnp.where(hit, row[k : k + 1, :], rows)
        scales = jnp.where(hit, scale[k : k + 1, :], scales)
    earlier = (iota((batch, batch), 0) < iota((batch, batch), 1)).astype(bf16)
    before = jnp.dot(named.astype(bf16), earlier, preferred_element_type=f32)
    place = jnp.where(named > 0, before + 1.0, 0.0)
    place_ref[...] = place
    scale_ref[...] = scales
    lanes = iota((devices, capacity), 1)
    asks = jnp.zeros((devices, capacity), f32)
    for s in range(capacity):
        col = jnp.sum(jnp.where(place == s + 1.0, rows, 0.0), axis=1, keepdims=True)
        asks = jnp.where(lanes == s, col, asks)
    asks_ref[...] = asks.astype(i32)


def route(own, row, expo, devices, capacity):
    batch = own.shape[1]
    return pl.pallas_call(
        route_kernel,
        out_shape=(
            jax.ShapeDtypeStruct((devices, capacity), i32),
            jax.ShapeDtypeStruct((devices, batch), f32),
            jax.ShapeDtypeStruct((devices, batch), f32),
        ),
        in_specs=[VM] * 3,
        out_specs=(VM,) * 3,
        compiler_params=PARAMS,
        name="route",
    )(own, row, expo)


def spread_kernel(place_ref, scale_ref, out_ref):
    devices, batch = place_ref.shape
    capacity = out_ref.shape[0] // devices
    full = (devices, capacity, batch)
    slots = (iota(full, 1) + 1).astype(f32)
    place = jnp.broadcast_to(place_ref[...][:, None, :], full)
    scale = jnp.broadcast_to(scale_ref[...][:, None, :], full)
    out = jnp.where(place == slots, scale, 0.0)
    out_ref[...] = out.reshape(devices * capacity, batch).astype(bf16)


def spread(place, scale, capacity):
    devices, batch = place.shape
    return pl.pallas_call(
        spread_kernel,
        out_shape=jax.ShapeDtypeStruct((devices * capacity, batch), bf16),
        in_specs=[VM] * 2,
        out_specs=VM,
        compiler_params=PARAMS,
        name="spread",
    )(place, scale)


def lookup_kernel(asked_ref, table_ref, out_ref):
    devices, capacity = asked_ref.shape
    slots, width = out_ref.shape
    rows = table_ref.shape[0]
    full = (devices, capacity, capacity)
    wide = jnp.broadcast_to(asked_ref[...].astype(f32)[:, None, :], full)
    kept = jnp.where(iota(full, 1) == iota(full, 2), wide, 0.0).reshape(slots, capacity)
    col = jnp.sum(kept, axis=1, keepdims=True).astype(i32)
    step = 256
    for at in range(0, slots, step):
        hit = col[at : at + step] == iota((step, rows), 1)
        onehot = jnp.where(hit, 1.0, 0.0).astype(bf16)
        got = jnp.dot(onehot, table_ref[...], preferred_element_type=f32)
        out_ref[at : at + step, :] = got.astype(bf16)


def lookup(asked, table):
    devices, capacity = asked.shape
    return pl.pallas_call(
        lookup_kernel,
        out_shape=jax.ShapeDtypeStruct((devices * capacity, table.shape[1]), bf16),
        in_specs=[VM] * 2,
        out_specs=VM,
        compiler_params=PARAMS,
        name="lookup",
    )(asked, table)


def contract_rows(a, b):
    return lax.dot_general(a, b, (((0,), (0,)), ((), ())), preferred_element_type=f32)


def tower_kernel(
    feat_ref, w_ref, head_ref, label_ref, ids_ref, spread_ref, out_ref, load_ref, pre_ref, sig_ref
):
    batch, din = feat_ref.shape
    parts, _, part = w_ref.shape
    width = din // 2
    keys = ids_ref.shape[1]
    feat = feat_ref[...]
    logit = jnp.zeros((batch, 1), f32)
    for t in range(parts):
        cols = slice(t * part, (t + 1) * part)
        pre = jnp.dot(feat, w_ref[t], preferred_element_type=f32)
        sig = jax.nn.sigmoid(pre)
        pre_ref[:, cols] = pre
        sig_ref[:, cols] = sig
        logit += jnp.sum(pre * sig * head_ref[:, cols], axis=1, keepdims=True)
    dlogit = jax.nn.sigmoid(logit) - label_ref[...]
    dfeat = jnp.zeros((batch, din), f32)
    for t in range(parts):
        cols = slice(t * part, (t + 1) * part)
        pre = pre_ref[:, cols]
        sig = sig_ref[:, cols]
        dpre = (dlogit * head_ref[:, cols] * sig * (1.0 + pre * (1.0 - sig))).astype(bf16)
        dfeat += lax.dot_general(
            dpre, w_ref[t], (((1,), (1,)), ((), ())), preferred_element_type=f32
        )
    dhot = dfeat[:, :width]
    dcold = dfeat[:, width:].astype(bf16)
    out_ref[...] = jnp.dot(spread_ref[...], dcold, preferred_element_type=f32).astype(bf16)
    hot_hi = dhot.astype(bf16)
    hot_lo = (dhot - hot_hi.astype(f32)).astype(bf16)
    load_ref[:, :din] = feat
    load_ref[:, din : din + width] = hot_hi
    load_ref[:, din + width : din + 2 * width] = hot_lo
    first = dlogit.astype(bf16).astype(f32)
    second = (dlogit - first).astype(bf16).astype(f32)
    third = dlogit - first - second
    lanes = iota((batch, 128), 1)
    extra = jnp.where(lanes == 0, first, 0.0)
    extra = jnp.where(lanes == 1, second, extra)
    extra = jnp.where(lanes == 2, third, extra)
    ids = ids_ref[...]
    high = lax.shift_right_logical(ids, 6)
    low = ids - high * 64
    high = high.astype(f32)
    low = low.astype(f32)
    for k in range(keys):
        extra = jnp.where(lanes == 8 + k, high[:, k : k + 1], extra)
        extra = jnp.where(lanes == 8 + keys + k, low[:, k : k + 1], extra)
    load_ref[:, din + 2 * width :] = extra.astype(bf16)


def tower(feat, w_parts, head, label, ids, spread_mat):
    batch, din = feat.shape
    hidden = w_parts.shape[0] * w_parts.shape[2]
    return pl.pallas_call(
        tower_kernel,
        out_shape=(
            jax.ShapeDtypeStruct((spread_mat.shape[0], din // 2), bf16),
            jax.ShapeDtypeStruct((batch, 2 * din + 128), bf16),
        ),
        in_specs=[VM] * 6,
        out_specs=(VM,) * 2,
        scratch_shapes=[pltpu.VMEM((batch, hidden), f32), pltpu.VMEM((batch, hidden), f32)],
        compiler_params=PARAMS,
        name="tower",
    )(feat, w_parts, head, label, ids, spread_mat)


def columns_kernel(keys, base_ref, load_ref, w_ref, head_ref, out_ref):
    samples = load_ref.shape[0]
    din, part = w_ref.shape
    width = din // 2
    rows = out_ref.shape[0]
    feat = load_ref[:, :din]
    extra = load_ref[:, 2 * din :].astype(f32)
    dlogit = extra[:, 0:1] + extra[:, 1:2] + extra[:, 2:3]
    pre = jnp.dot(feat, w_ref[...], preferred_element_type=f32)
    sig = jax.nn.sigmoid(pre)
    dpre = (dlogit * head_ref[...] * sig * (1.0 + pre * (1.0 - sig))).astype(bf16)
    out_ref[:, :part] = contract_rows(feat, dpre).astype(bf16)
    lanes = (iota((samples, rows), 1) + base_ref[0]).astype(f32)
    counts = jnp.zeros((samples, rows), f32)
    for k in range(keys):
        ids = extra[:, 8 + k : 9 + k] * 64.0 + extra[:, 8 + keys + k : 9 + keys + k]
        counts += jnp.where(ids == lanes, 1.0, 0.0)
    counts = counts.astype(bf16)
    hot = contract_rows(counts, load_ref[:, din : din + width])
    hot += contract_rows(counts, load_ref[:, din + width : 2 * din])
    out_ref[:, part:] = hot.astype(bf16)


def columns(load, w_half, head, base, keys, rows):
    din, part = w_half.shape
    return pl.pallas_call(
        lambda *refs: columns_kernel(keys, *refs),
        out_shape=jax.ShapeDtypeStruct((rows, part + din // 2), bf16),
        in_specs=[pl.BlockSpec(memory_space=pltpu.SMEM)] + [VM] * 3,
        out_specs=VM,
        compiler_params=PARAMS,
        name="columns",
    )(base, load, w_half, head)


def cold_kernel(asked_ref, grads_ref, table_ref, acc_ref, new_ref, new_acc_ref):
    step, width = table_ref.shape
    slots = grads_ref.shape[0]
    rows = iota((step, slots), 0) + pl.program_id(0) * step
    onehot = jnp.where(asked_ref[...] == rows, 1.0, 0.0).astype(bf16)
    grad = jnp.dot(onehot, grads_ref[...], preferred_element_type=f32)
    param, acc = adagrad(table_ref[...], acc_ref[...], grad)
    new_ref[...] = param
    new_acc_ref[...] = acc


def cold_update(asked, grads, table, acc):
    rows, width = table.shape
    slots = grads.shape[0]
    step = 256
    block = pl.BlockSpec((step, width), lambda i: (i, 0))
    return pl.pallas_call(
        cold_kernel,
        grid=(rows // step,),
        out_shape=(jax.ShapeDtypeStruct(table.shape, f32),) * 2,
        in_specs=[
            pl.BlockSpec((1, slots), lambda i: (0, 0)),
            pl.BlockSpec((slots, width), lambda i: (0, 0)),
            block,
            block,
        ],
        out_specs=(block, block),
        compiler_params=PARAMS,
        name="cold_update",
    )(asked, grads, table, acc)


def on_device(
    hot_ids,
    cold_owner,
    cold_row,
    cold_exp,
    labels,
    head_w,
    hot_table,
    hot_acc,
    cold_table,
    cold_acc,
    tower_w,
    tower_acc,
):
    devices = lax.axis_size("table") * lax.axis_size("replica")
    replicas = lax.axis_size("replica")
    me = lax.axis_index("table")
    batch, keys = hot_ids.shape
    hot_rows, width = hot_table.shape
    part = tower_w.shape[1]
    capacity = max(2, 2 * batch * cold_owner.shape[1] // devices)
    w_half = tower_w.astype(bf16)
    w_parts = lax.all_gather(w_half, "table", axis=0)
    all_hot = lax.all_gather(hot_table.astype(bf16), "table", axis=0, tiled=True)

    asks, place, scale = route(cold_owner.T, cold_row.T, cold_exp.T, devices, capacity)
    asked = lax.all_to_all(asks, ALL, split_axis=0, concat_axis=0, tiled=True)
    spread_mat = spread(place, scale, capacity)
    looked = lookup(asked, cold_table.astype(bf16))
    returned = lax.all_to_all(
        looked.reshape(devices, capacity, width), ALL, split_axis=0, concat_axis=0, tiled=True
    ).reshape(-1, width)

    counts = jnp.sum(
        (hot_ids[:, :, None] == jnp.arange(all_hot.shape[0], dtype=i32)[None, None, :]).astype(f32),
        axis=1,
    ).astype(bf16)
    hot_pool = jnp.dot(counts, all_hot, preferred_element_type=f32)
    cold_pool = contract_rows(spread_mat, returned)
    feat = jnp.concatenate([hot_pool, cold_pool], axis=1).astype(bf16)
    outgoing, load = tower(
        feat, w_parts, head_w[None, :], labels[:, None], hot_ids, spread_mat
    )
    loads = lax.all_gather(load, "table", axis=0, tiled=True)
    incoming = lax.all_to_all(
        outgoing.reshape(devices, capacity, width), ALL, split_axis=0, concat_axis=0, tiled=True
    ).reshape(-1, width)

    head_part = lax.dynamic_slice(head_w, (me * part,), (part,))[None, :]
    base = (me * hot_rows).astype(i32)[None]
    partial = columns(loads, w_half, head_part, base, keys, hot_rows)
    terms = lax.all_to_all(partial, "replica", split_axis=0, concat_axis=0, tiled=True)
    piece = jnp.sum(terms.reshape(replicas, -1, part + width).astype(f32), axis=0)
    copies = jnp.broadcast_to(piece[None], (replicas,) + piece.shape)
    grads = lax.all_to_all(copies, "replica", split_axis=0, concat_axis=0, tiled=True)
    grads = grads.reshape(hot_rows, part + width)

    new_cold, new_cold_acc = cold_update(asked.reshape(1, -1), incoming, cold_table, cold_acc)
    new_hot, new_hot_acc = adagrad(hot_table, hot_acc, grads[:, part:])
    new_w, new_w_acc = adagrad(tower_w, tower_acc, grads[:, :part])
    return (new_hot, new_hot_acc, new_cold, new_cold_acc, new_w, new_w_acc)


def solution(mesh):
    split = P(ALL, None)
    return jax.shard_map(
        on_device,
        mesh=mesh,
        in_specs=(
            split,
            split,
            split,
            split,
            P(ALL),
            P(),
            P("table", None),
            P("table", None),
            split,
            split,
            P(None, "table"),
            P(None, "table"),
        ),
        out_specs=(
            P("table", None),
            P("table", None),
            split,
            split,
            P(None, "table"),
            P(None, "table"),
        ),
        check_vma=False,
    )
```

```python
import functools
import math

import jax
import jax.numpy as jnp
from jax import lax
from jax.experimental import pallas as pl
from jax.experimental.pallas import tpu as pltpu
from jax.sharding import PartitionSpec as P

learn_rate = 0.05
bf16 = jnp.bfloat16
f32 = jnp.float32
i32 = jnp.int32
ALL = ("y", "core", "z", "x")
TABLE = ("y", "core")
VM = pl.BlockSpec(memory_space=pltpu.VMEM)
HBM = pl.BlockSpec(memory_space=pltpu.HBM)
MIB = 1024 * 1024
PARAMS = pltpu.CompilerParams(vmem_limit_bytes=24 * MIB)
ALONE = pltpu.CompilerParams(vmem_limit_bytes=60 * MIB)


def adagrad(param, accum, grad):
    new_accum = accum + grad * grad
    return (param - learn_rate * grad * lax.rsqrt(new_accum), new_accum)


def cost(us):
    return pl.CostEstimate(flops=int(us * 1e9), bytes_accessed=int(us * 3e6), transcendentals=0)


def iota(shape, axis):
    return lax.broadcasted_iota(i32, shape, axis)


def route_kernel(
    own_hbm,
    row_hbm,
    exp_hbm,
    hot_hbm,
    w_hbm,
    asks_ref,
    place_ref,
    scale_ref,
    half_ref,
    quarter_ref,
    own_ref,
    row_ref,
    exp_ref,
    hot_ref,
    w_ref,
    sems,
):
    pairs = (
        (own_hbm, own_ref),
        (row_hbm, row_ref),
        (exp_hbm, exp_ref),
        (hot_hbm, hot_ref),
        (w_hbm, w_ref),
    )
    copies = [pltpu.make_async_copy(a, b, sems.at[n]) for n, (a, b) in enumerate(pairs)]
    for copy in copies:
        copy.start()
    for copy in copies[:3]:
        copy.wait()
    keys, batch = own_ref.shape
    devices, capacity = asks_ref.shape
    owners = iota((devices, batch), 0)
    named = jnp.zeros((devices, batch), f32)
    rows = jnp.zeros((devices, batch), f32)
    scales = jnp.zeros((devices, batch), f32)
    expo = exp_ref[...]
    scale = jnp.where(expo == 0, 1.0, jnp.where(expo == 1, 0.5, 0.25))
    row = row_ref[...].astype(f32)
    own = own_ref[...]
    for k in range(keys):
        hit = own[k : k + 1, :] == owners
        named = jnp.where(hit, 1.0, named)
        rows = jnp.where(hit, row[k : k + 1, :], rows)
        scales = jnp.where(hit, scale[k : k + 1, :], scales)
    earlier = (iota((batch, batch), 0) < iota((batch, batch), 1)).astype(bf16)
    before = jnp.dot(named.astype(bf16), earlier, preferred_element_type=f32)
    place = jnp.where(named > 0, before + 1.0, 0.0)
    place_ref[...] = place
    scale_ref[...] = scales
    lanes = iota((devices, capacity), 1)
    asks = jnp.zeros((devices, capacity), f32)
    for s in range(capacity):
        col = jnp.sum(jnp.where(place == s + 1.0, rows, 0.0), axis=1, keepdims=True)
        asks = jnp.where(lanes == s, col, asks)
    asks_ref[...] = asks.astype(i32)
    din, rows_hot, width = w_ref.shape[0], hot_ref.shape[0] // 2, hot_ref.shape[1]
    copies[3].wait()
    half_ref[din:, :width] = hot_ref[:rows_hot, :].astype(bf16)
    half_ref[din:, width:] = hot_ref[rows_hot:, :].astype(bf16)
    copies[4].wait()
    half_ref[:din, :] = w_ref[...].astype(bf16)
    for which, axis in ((0, "x"), (1, "z")):
        at = lax.axis_index(axis)
        for first, count, to in ((0, din // 8, 0), (din, rows_hot // 8, din // 8)):
            start = pl.multiple_of(first + which * 4 * count + at * count, count)
            to += which * (din + rows_hot) // 8
            quarter_ref[to : to + count, :] = half_ref[pl.ds(start, count), :]


def route(own, row, expo, hot, w, devices, capacity):
    batch = own.shape[1]
    return pl.pallas_call(
        route_kernel,
        out_shape=(
            jax.ShapeDtypeStruct((devices, capacity), i32),
            jax.ShapeDtypeStruct((devices, batch), f32),
            jax.ShapeDtypeStruct((devices, batch), f32),
            jax.ShapeDtypeStruct((w.shape[0] + hot.shape[0] // 2, w.shape[1]), bf16),
            jax.ShapeDtypeStruct((w.shape[0] // 4 + hot.shape[0] // 8, w.shape[1]), bf16),
        ),
        in_specs=[HBM] * 5,
        out_specs=(VM,) * 5,
        scratch_shapes=[
            pltpu.VMEM(own.shape, i32),
            pltpu.VMEM(row.shape, i32),
            pltpu.VMEM(expo.shape, i32),
            pltpu.VMEM(hot.shape, f32),
            pltpu.VMEM(w.shape, f32),
            pltpu.SemaphoreType.DMA((5,)),
        ],
        compiler_params=ALONE,
        cost_estimate=cost(2),
        name="route",
    )(own, row, expo, hot, w)


def spread_kernel(place_ref, scale_ref, out_hbm, out_ref, sem):
    devices, batch = place_ref.shape
    capacity = out_ref.shape[0] // devices
    full = (devices, capacity, batch)
    slots = (iota(full, 1) + 1).astype(f32)
    place = jnp.broadcast_to(place_ref[...][:, None, :], full)
    scale = jnp.broadcast_to(scale_ref[...][:, None, :], full)
    out = jnp.where(place == slots, scale, 0.0)
    out_ref[...] = out.reshape(devices * capacity, batch).astype(bf16)
    copy = pltpu.make_async_copy(out_ref, out_hbm, sem)
    copy.start()
    copy.wait()


def spread(place, scale, capacity):
    devices, batch = place.shape
    shape = (devices * capacity, batch)
    return pl.pallas_call(
        spread_kernel,
        out_shape=jax.ShapeDtypeStruct(shape, bf16),
        in_specs=[VM] * 2,
        out_specs=HBM,
        scratch_shapes=[pltpu.VMEM(shape, bf16), pltpu.SemaphoreType.DMA],
        compiler_params=ALONE,
        cost_estimate=cost(1),
        name="spread",
    )(place, scale)


def lookup_kernel(asked_ref, table_hbm, out_hbm, table_ref, half_ref, out_ref, in_sems, sems):
    devices, capacity = asked_ref.shape
    slots, width = out_ref.shape
    rows = table_ref.shape[0]
    parts = in_sems.shape[0]
    loads = []
    for n in range(parts):
        at = slice(n * rows // parts, (n + 1) * rows // parts)
        loads.append(pltpu.make_async_copy(table_hbm.at[at], table_ref.at[at], in_sems.at[n]))
        loads[n].start()
    full = (devices, capacity, capacity)
    wide = jnp.broadcast_to(asked_ref[...].astype(f32)[:, None, :], full)
    kept = jnp.where(iota(full, 1) == iota(full, 2), wide, 0.0).reshape(slots, capacity)
    col = jnp.sum(kept, axis=1, keepdims=True).astype(i32)
    for n in range(parts):
        at = slice(n * rows // parts, (n + 1) * rows // parts)
        loads[n].wait()
        half_ref[at, :] = table_ref[at, :].astype(bf16)
    step = 256
    copies = []
    for at in range(0, slots, step):
        hit = col[at : at + step] == iota((step, rows), 1)
        onehot = jnp.where(hit, 1.0, 0.0).astype(bf16)
        got = jnp.dot(onehot, half_ref[...], preferred_element_type=f32)
        out_ref[at : at + step, :] = got.astype(bf16)
        copies.append(
            pltpu.make_async_copy(
                out_ref.at[at : at + step], out_hbm.at[at : at + step], sems.at[at // step]
            )
        )
        copies[-1].start()
    for copy in copies:
        copy.wait()


def lookup(asked, table):
    devices, capacity = asked.shape
    shape = (devices * capacity, table.shape[1])
    return pl.pallas_call(
        lookup_kernel,
        out_shape=jax.ShapeDtypeStruct(shape, bf16),
        in_specs=[VM, HBM],
        out_specs=HBM,
        scratch_shapes=[
            pltpu.VMEM(table.shape, f32),
            pltpu.VMEM(table.shape, bf16),
            pltpu.VMEM(shape, bf16),
            pltpu.SemaphoreType.DMA((4,)),
            pltpu.SemaphoreType.DMA((shape[0] // 256,)),
        ],
        compiler_params=ALONE,
        cost_estimate=cost(3),
        name="lookup",
    )(asked, table)


def contract_rows(a, b):
    return lax.dot_general(a, b, (((0,), (0,)), ((), ())), preferred_element_type=f32)


def gather_copies(refs, first, buf, sems):
    x, z = lax.axis_index("x"), lax.axis_index("z")
    rows = buf.shape[1]
    count = rows // 8
    lists = []
    n = 0
    for side in range(2):
        half, *others = refs[9 * side : 9 * side + 9]
        piece = others[0].shape[0] // 3
        for dy in range(4):
            t = 4 * side + dy
            moves = [] if dy else [(half, first, 0, rows)]
            for which, at in ((0, x), (1, z)) if dy else ():
                for d in range(4):
                    to = lax.rem(at + d, 4) * count + which * 4 * count
                    start = (dy - 1) * piece + first // 8
                    moves.append((others[4 * which + d], start, to, count))
            copies = []
            for src, start, to, size in moves:
                to_rows = pl.ds(pl.multiple_of(to, count), size)
                copies.append(
                    pltpu.make_async_copy(
                        src.at[start : start + size], buf.at[t, to_rows], sems.at[n]
                    )
                )
                n += 1
            lists.append(copies)
    return lists


COPIES = 2 * (1 + 3 * 8)


def hot_pool_kernel(ids_ref, *refs):
    refs, (out_ref, buf, sems) = refs[:-3], refs[-3:]
    batch, keys = ids_ref.shape
    _, rows, wide = buf.shape
    width = out_ref.shape[1]
    lists = gather_copies(refs, refs[0].shape[0] - rows, buf, sems)
    for copies in lists:
        for copy in copies:
            copy.start()
    y, core = lax.axis_index("y"), lax.axis_index("core")
    ids = ids_ref[...]
    pool = jnp.zeros((batch, width), f32)
    for t, copies in enumerate(lists):
        side = core if t < 4 else 1 - core
        first = (2 * lax.rem(y + t, 4) + side) * 2 * rows
        lanes = iota((batch, 2 * rows), 1) + first
        counts = jnp.zeros((batch, 2 * rows), f32)
        for k in range(keys):
            counts += jnp.where(ids[:, k : k + 1] == lanes, 1.0, 0.0)
        counts = counts.astype(bf16)
        for copy in copies:
            copy.wait()
        pool += jnp.dot(counts[:, :rows], buf[t, :, :width], preferred_element_type=f32)
        pool += jnp.dot(counts[:, rows:], buf[t, :, width:], preferred_element_type=f32)
    out_ref[...] = pool.astype(bf16)


def hot_pooled(ids, pieces, width):
    wide = pieces[0].shape[1]
    rows = pieces[0].shape[0] - 2 * width
    return pl.pallas_call(
        hot_pool_kernel,
        out_shape=jax.ShapeDtypeStruct((ids.shape[0], width), bf16),
        in_specs=[VM] + [HBM] * len(pieces),
        out_specs=VM,
        scratch_shapes=[pltpu.VMEM((8, rows, wide), bf16), pltpu.SemaphoreType.DMA((COPIES,))],
        compiler_params=ALONE,
        cost_estimate=cost(0.1),
        name="hot_pool",
    )(ids, *pieces)


def tower_kernel(
    hot_ref,
    head_ref,
    label_ref,
    ids_ref,
    returned_hbm,
    spread_hbm,
    *refs,
):
    pieces, refs = refs[:-9], refs[-9:]
    dcold_ref, load_ref, pre_ref, sig_ref, returned_ref, spread_ref, w_ref, two, sems = refs
    batch, width = hot_ref.shape
    parts, din, part = w_ref.shape
    keys = ids_ref.shape[1]
    firsts = [
        pltpu.make_async_copy(spread_hbm, spread_ref, two.at[0]),
        pltpu.make_async_copy(returned_hbm, returned_ref, two.at[1]),
    ]
    lists = gather_copies(pieces, 0, w_ref, sems)
    for copies in [firsts] + lists:
        for copy in copies:
            copy.start()
    for copy in firsts:
        copy.wait()
    cold = contract_rows(spread_ref[...], returned_ref[...]).astype(bf16)
    feat = jnp.concatenate([hot_ref[...], cold], axis=1)
    logit = jnp.zeros((batch, 1), f32)
    for t in range(parts):
        cols = slice(t * part, (t + 1) * part)
        for copy in lists[t]:
            copy.wait()
        pre = jnp.dot(feat, w_ref[t], preferred_element_type=f32)
        sig = jax.nn.sigmoid(pre)
        pre_ref[:, cols] = pre
        sig_ref[:, cols] = sig
        logit += jnp.sum(pre * sig * head_ref[:, cols], axis=1, keepdims=True)
    dlogit = jax.nn.sigmoid(logit) - label_ref[...]
    dfeat = jnp.zeros((batch, din), f32)
    for t in range(parts):
        cols = slice(t * part, (t + 1) * part)
        pre = pre_ref[:, cols]
        sig = sig_ref[:, cols]
        dpre = (dlogit * head_ref[:, cols] * sig * (1.0 + pre * (1.0 - sig))).astype(bf16)
        dfeat += lax.dot_general(
            dpre, w_ref[t], (((1,), (1,)), ((), ())), preferred_element_type=f32
        )
    dhot = dfeat[:, :width]
    dcold_ref[...] = dfeat[:, width:].astype(bf16)
    hot_hi = dhot.astype(bf16)
    hot_lo = (dhot - hot_hi.astype(f32)).astype(bf16)
    load_ref[:, :din] = feat
    load_ref[:, din : din + width] = hot_hi
    load_ref[:, din + width : 2 * din] = hot_lo
    first = dlogit.astype(bf16).astype(f32)
    second = (dlogit - first).astype(bf16).astype(f32)
    third = dlogit - first - second
    lanes = iota((batch, 128), 1)
    extra = jnp.where(lanes == 0, first, 0.0)
    extra = jnp.where(lanes == 1, second, extra)
    extra = jnp.where(lanes == 2, third, extra)
    ids = ids_ref[...]
    high = lax.shift_right_logical(ids, 6)
    low = ids - high * 64
    high = high.astype(f32)
    low = low.astype(f32)
    for k in range(keys):
        extra = jnp.where(lanes == 8 + k, high[:, k : k + 1], extra)
        extra = jnp.where(lanes == 8 + keys + k, low[:, k : k + 1], extra)
    load_ref[:, 2 * din :] = extra.astype(bf16)


def tower(hot, returned, spread_mat, head, label, ids, pieces):
    batch, width = hot.shape
    hidden = head.shape[1]
    return pl.pallas_call(
        tower_kernel,
        out_shape=(
            jax.ShapeDtypeStruct((batch, width), bf16),
            jax.ShapeDtypeStruct((batch, 4 * width + 128), bf16),
        ),
        in_specs=[VM] * 4 + [HBM] * (2 + len(pieces)),
        out_specs=(VM, VM),
        scratch_shapes=[
            pltpu.VMEM((batch, hidden), f32),
            pltpu.VMEM((batch, hidden), f32),
            pltpu.VMEM(returned.shape, bf16),
            pltpu.VMEM(spread_mat.shape, bf16),
            pltpu.VMEM((8, 2 * width, hidden // 8), bf16),
            pltpu.SemaphoreType.DMA((2,)),
            pltpu.SemaphoreType.DMA((COPIES,)),
        ],
        compiler_params=ALONE,
        cost_estimate=cost(6),
        name="tower",
    )(hot, head, label, ids, returned, spread_mat, *pieces)


def outgoing_kernel(dcold_ref, spread_hbm, out_hbm, spread_ref, out_ref, sems):
    slots = spread_ref.shape[0]
    step = slots // 4
    loads = []
    for n in range(4):
        at = slice(n * step, (n + 1) * step)
        loads.append(pltpu.make_async_copy(spread_hbm.at[at], spread_ref.at[at], sems.at[n]))
        loads[n].start()
    stores = []
    for n in range(4):
        at = slice(n * step, (n + 1) * step)
        loads[n].wait()
        out = jnp.dot(spread_ref[at, :], dcold_ref[...], preferred_element_type=f32)
        out_ref[at, :] = out.astype(bf16)
        stores.append(pltpu.make_async_copy(out_ref.at[at], out_hbm.at[at], sems.at[4 + n]))
        stores[n].start()
    for store in stores:
        store.wait()


def outgoing_of(dcold, spread_mat):
    shape = (spread_mat.shape[0], dcold.shape[1])
    return pl.pallas_call(
        outgoing_kernel,
        out_shape=jax.ShapeDtypeStruct(shape, bf16),
        in_specs=[VM, HBM],
        out_specs=HBM,
        scratch_shapes=[
            pltpu.VMEM(spread_mat.shape, bf16),
            pltpu.VMEM(shape, bf16),
            pltpu.SemaphoreType.DMA((8,)),
        ],
        compiler_params=ALONE,
        cost_estimate=cost(30),
        name="outgoing",
    )(dcold, spread_mat)


def columns_kernel(keys, head_ref, half_hbm, *refs):
    loads, (out_ref, half_ref, load_ref, sems) = refs[:-4], refs[-4:]
    din, part = half_ref.shape
    rows, width = din, din // 2
    batch = loads[0].shape[0]
    first = pltpu.make_async_copy(half_hbm.at[:din], half_ref, sems.at[len(loads)])
    copies = [
        pltpu.make_async_copy(ref, load_ref.at[pl.ds(n * batch, batch)], sems.at[n])
        for n, ref in enumerate(loads)
    ]
    for copy in [first] + copies:
        copy.start()
    first.wait()
    base = (2 * lax.axis_index("y") + lax.axis_index("core")) * rows
    lanes = (iota((2 * batch, rows), 1) + base).astype(f32)
    tower_grad = jnp.zeros((din, part), f32)
    hot_grad = jnp.zeros((rows, width), f32)
    for n in range(0, len(loads), 2):
        copies[n].wait()
        copies[n + 1].wait()
        at = slice(n * batch, (n + 2) * batch)
        feat = load_ref[at, :din]
        extra = load_ref[at, 2 * din :].astype(f32)
        dlogit = extra[:, 0:1] + extra[:, 1:2] + extra[:, 2:3]
        pre = jnp.dot(feat, half_ref[...], preferred_element_type=f32)
        sig = jax.nn.sigmoid(pre)
        dpre = (dlogit * head_ref[...] * sig * (1.0 + pre * (1.0 - sig))).astype(bf16)
        tower_grad += contract_rows(feat, dpre)
        counts = jnp.zeros((2 * batch, rows), f32)
        for k in range(keys):
            ids = extra[:, 8 + k : 9 + k] * 64.0 + extra[:, 8 + keys + k : 9 + keys + k]
            counts += jnp.where(ids == lanes, 1.0, 0.0)
        counts = counts.astype(bf16)
        hot_grad += contract_rows(counts, load_ref[at, din : din + width])
        hot_grad += contract_rows(counts, load_ref[at, din + width : 2 * din])
    out_ref[:, :part] = tower_grad.astype(bf16)
    out_ref[:, part:] = hot_grad.astype(bf16)


def columns(loads, half, head, keys):
    batch, wide = loads[0].shape
    return pl.pallas_call(
        functools.partial(columns_kernel, keys),
        out_shape=jax.ShapeDtypeStruct((half.shape[1], half.shape[0]), bf16),
        in_specs=[VM] + [HBM] * (1 + len(loads)),
        out_specs=VM,
        scratch_shapes=[
            pltpu.VMEM((half.shape[1], half.shape[1]), bf16),
            pltpu.VMEM((batch * len(loads), wide), bf16),
            pltpu.SemaphoreType.DMA((1 + len(loads),)),
        ],
        compiler_params=ALONE,
        cost_estimate=cost(5),
        name="columns",
    )(head, half, *loads)


def total_kernel(terms_ref, left_ref, right_ref):
    total = terms_ref[0].astype(f32)
    for n in range(1, terms_ref.shape[0]):
        total += terms_ref[n].astype(f32)
    half = left_ref.shape[1]
    left_ref[...] = total[:, :half]
    right_ref[...] = total[:, half:]


def total_of(terms):
    _, rows, wide = terms.shape
    return pl.pallas_call(
        total_kernel,
        out_shape=(jax.ShapeDtypeStruct((rows, wide // 2), f32),) * 2,
        in_specs=[VM],
        out_specs=(VM,) * 2,
        compiler_params=PARAMS,
        cost_estimate=cost(1),
        name="total",
    )(terms)


def lay_kernel(*refs):
    out0, out1 = refs[-2:]
    for axis, parts, out in (("z", refs[:4], out0), ("x", refs[4:8], out1)):
        step = parts[0].shape[0]
        for n, ref in enumerate(parts):
            at = lax.rem(lax.axis_index(axis) + n, 4) * step
            out[pl.ds(pl.multiple_of(at, step), step), :] = ref[...]


def lay(left, right):
    rows, wide = left[0].shape
    return pl.pallas_call(
        lay_kernel,
        out_shape=(jax.ShapeDtypeStruct((4 * rows, wide), f32),) * 2,
        in_specs=[VM] * 8,
        out_specs=(VM,) * 2,
        compiler_params=PARAMS,
        cost_estimate=cost(1),
        name="lay",
    )(*left, *right)


def update_kernel(l0, l1, l2, l3, r0, r1, r2, r3, *refs):
    w_ref, w_acc_ref, hot_ref, hot_acc_ref, nw_ref, nwa_ref, nh_ref, nha_ref, grad_ref = refs
    part = w_ref.shape[1]
    step, half = l0.shape
    piece = step // 4
    i = pl.program_id(0)
    for d, left in enumerate((l0, l1, l2, l3)):

        @pl.when(lax.rem(lax.axis_index("x") + d, 4) == i)
        def _():
            grad_ref[:, :half] = left[...]

    start = pl.multiple_of(i * piece, piece)
    for d, right in enumerate((r0, r1, r2, r3)):
        at = lax.rem(lax.axis_index("z") + d, 4) * piece
        grad_ref[pl.ds(pl.multiple_of(at, piece), piece), half:] = right[pl.ds(start, piece), :]
    nw, nwa = adagrad(w_ref[...], w_acc_ref[...], grad_ref[:, :part])
    nw_ref[...] = nw
    nwa_ref[...] = nwa
    nh, nha = adagrad(hot_ref[...], hot_acc_ref[...], grad_ref[:, part:])
    nh_ref[...] = nh
    nha_ref[...] = nha


def update(left, right, w, w_acc, hot, hot_acc):
    step, half = left[0].shape
    w_block = pl.BlockSpec((step, w.shape[1]), lambda i: (i, 0))
    hot_block = pl.BlockSpec((step, hot.shape[1]), lambda i: (i, 0))
    return pl.pallas_call(
        update_kernel,
        grid=(4,),
        in_specs=[VM] * 8
        + [w_block] * 2
        + [hot_block] * 2,
        out_specs=(w_block, w_block, hot_block, hot_block),
        out_shape=(jax.ShapeDtypeStruct(w.shape, f32),) * 2
        + (jax.ShapeDtypeStruct(hot.shape, f32),) * 2,
        scratch_shapes=[pltpu.VMEM((step, 2 * half), f32)],
        compiler_params=ALONE,
        cost_estimate=cost(4),
        name="update",
    )(*left, *right, w, w_acc, hot, hot_acc)


def cold_kernel(asked_ref, grads_ref, table_ref, acc_ref, new_ref, new_acc_ref):
    step, width = table_ref.shape
    slots = grads_ref.shape[0]
    rows = iota((step, slots), 0) + pl.program_id(0) * step
    onehot = jnp.where(asked_ref[...] == rows, 1.0, 0.0).astype(bf16)
    grad = jnp.dot(onehot, grads_ref[...], preferred_element_type=f32)
    param, acc = adagrad(table_ref[...], acc_ref[...], grad)
    new_ref[...] = param
    new_acc_ref[...] = acc


def cold_update(asked, grads, table, acc):
    rows, width = table.shape
    slots = grads.shape[0]
    step = 256
    block = pl.BlockSpec((step, width), lambda i: (i, 0))
    return pl.pallas_call(
        cold_kernel,
        grid=(rows // step,),
        out_shape=(jax.ShapeDtypeStruct(table.shape, f32),) * 2,
        in_specs=[
            pl.BlockSpec((1, slots), lambda i: (0, 0)),
            pl.BlockSpec((slots, width), lambda i: (0, 0)),
            block,
            block,
        ],
        out_specs=(block, block),
        compiler_params=PARAMS,
        cost_estimate=cost(5),
        name="cold_update",
    )(asked, grads, table, acc)


def along(value, axis, by):
    return lax.ppermute(value, axis, [((i + by) % 4, i) for i in range(4)])


def around(value, axis):
    last, one = along(value, axis, 3), along(value, axis, 1)
    return value, one, along(value, axis, 2), last


def swap(value):
    return lax.ppermute(value, "core", [(0, 1), (1, 0)])


def on_device(
    hot_ids,
    cold_owner,
    cold_row,
    cold_exp,
    labels,
    head_w,
    hot_table,
    hot_acc,
    cold_table,
    cold_acc,
    tower_w,
    tower_acc,
):
    devices = math.prod(lax.axis_size(name) for name in ALL)
    y, core = lax.axis_index("y"), lax.axis_index("core")
    me = 2 * y + core
    batch, keys = hot_ids.shape
    hot_rows, width = hot_table.shape
    part = tower_w.shape[1]
    capacity = max(2, 2 * batch * cold_owner.shape[1] // devices)
    asks, place, scale, half, quarter = route(
        cold_owner.T, cold_row.T, cold_exp.T, hot_table, tower_w, devices, capacity
    )
    asked = lax.all_to_all(asks, ALL, split_axis=0, concat_axis=0, tiled=True)
    spread_mat = spread(place, scale, capacity)
    quarters = tuple(along(quarter, "y", by) for by in (1, 2, 3))
    asked, quarters = lax.optimization_barrier((asked, quarters))
    count = quarter.shape[0] // 2
    by_x = jnp.concatenate([value[:count] for value in quarters])
    by_z = jnp.concatenate([value[count:] for value in quarters])
    looked = lookup(asked, cold_table)
    xs = tuple(along(by_x, "x", by) for by in (1, 2, 3))
    zs = tuple(along(by_z, "z", by) for by in (1, 2, 3))
    returned = lax.all_to_all(
        looked.reshape(devices, capacity, width), ALL, split_axis=0, concat_axis=0, tiled=True
    ).reshape(-1, width)
    pieces = lax.optimization_barrier((half, by_x) + xs + (by_z,) + zs)
    pieces += tuple(swap(value) for value in pieces)
    hot_feat = hot_pooled(hot_ids, pieces, width)
    heads = head_w.reshape(4, 2, part)
    turned = jnp.concatenate([heads, heads])
    turned = lax.dynamic_slice_in_dim(turned, y, 4, 0)
    head = jnp.concatenate(
        [lax.dynamic_slice_in_dim(turned, side, 1, 1).reshape(1, -1) for side in (core, 1 - core)],
        axis=1,
    )
    dcold, load = tower(
        hot_feat, returned, spread_mat, head, labels[:, None], hot_ids, pieces
    )
    loads = around(load, "y")
    outgoing = outgoing_of(dcold, spread_mat)
    incoming = lax.all_to_all(
        outgoing.reshape(devices, capacity, width), ALL, split_axis=0, concat_axis=0, tiled=True
    ).reshape(-1, width)
    loads += tuple(swap(part) for part in loads)
    head_part = lax.dynamic_slice(head_w, (me * part,), (part,))[None, :]
    partial = columns(loads, half, head_part, keys)
    partial, incoming = lax.optimization_barrier((partial, incoming))
    terms = lax.all_to_all(partial, ("x", "z"), split_axis=0, concat_axis=0, tiled=True)
    new_cold = cold_update(asked.reshape(1, -1), incoming, cold_table, cold_acc)
    terms, (new_cold, new_cold_acc) = lax.optimization_barrier((terms, new_cold))
    left, right = total_of(terms.reshape(16, -1, part + width))
    left, right = lay(around(left, "z"), around(right, "x"))
    left, right = around(left, "x"), around(right, "z")
    new_w, new_w_acc, new_hot, new_hot_acc = update(
        left, right, tower_w, tower_acc, hot_table, hot_acc
    )
    return (new_hot, new_hot_acc, new_cold, new_cold_acc, new_w, new_w_acc)


def solution(mesh):
    chips = mesh.devices.reshape(4, 2, 4, 4)
    mesh = jax.sharding.Mesh(chips, ALL)
    split = P(ALL, None)
    rows = P(TABLE, None)
    cols = P(None, TABLE)
    return jax.shard_map(
        on_device,
        mesh=mesh,
        in_specs=(split,) * 4 + (P(ALL), P(), rows, rows, split, split, cols, cols),
        out_specs=(rows, rows, split, split, cols, cols),
        check_vma=False,
    )
```

```python
import functools
import math

import jax
import jax.numpy as jnp
from jax import lax
from jax.experimental import pallas as pl
from jax.experimental.pallas import tpu as pltpu
from jax.sharding import PartitionSpec as P

learn_rate = 0.05
bf16 = jnp.bfloat16
f32 = jnp.float32
i32 = jnp.int32
ALL = ("y", "core", "z", "x")
TABLE = ("y", "core")
VM = pl.BlockSpec(memory_space=pltpu.VMEM)
HBM = pl.BlockSpec(memory_space=pltpu.HBM)
MIB = 1024 * 1024
PARAMS = pltpu.CompilerParams(vmem_limit_bytes=24 * MIB)
MOST = pltpu.CompilerParams(vmem_limit_bytes=57 * MIB)
ALONE = pltpu.CompilerParams(vmem_limit_bytes=60 * MIB)


def adagrad(param, accum, grad):
    new_accum = accum + grad * grad
    return (param - learn_rate * grad * lax.rsqrt(new_accum), new_accum)


def cost(us):
    return pl.CostEstimate(flops=int(us * 1e9), bytes_accessed=int(us * 3e6), transcendentals=0)


def iota(shape, axis):
    return lax.broadcasted_iota(i32, shape, axis)


def route_kernel(
    own_hbm,
    row_hbm,
    exp_hbm,
    hot_hbm,
    w_hbm,
    asks_ref,
    place_ref,
    scale_ref,
    half_ref,
    quarter_ref,
    own_ref,
    row_ref,
    exp_ref,
    hot_ref,
    w_ref,
    sems,
):
    pairs = (
        (own_hbm, own_ref),
        (row_hbm, row_ref),
        (exp_hbm, exp_ref),
        (hot_hbm, hot_ref),
        (w_hbm, w_ref),
    )
    copies = [pltpu.make_async_copy(a, b, sems.at[n]) for n, (a, b) in enumerate(pairs)]
    for copy in copies:
        copy.start()
    for copy in copies[:3]:
        copy.wait()
    keys, batch = own_ref.shape
    devices, capacity = asks_ref.shape
    owners = iota((devices, batch), 0)
    named = jnp.zeros((devices, batch), f32)
    rows = jnp.zeros((devices, batch), f32)
    scales = jnp.zeros((devices, batch), f32)
    expo = exp_ref[...]
    scale = jnp.where(expo == 0, 1.0, jnp.where(expo == 1, 0.5, 0.25))
    row = row_ref[...].astype(f32)
    own = own_ref[...]
    for k in range(keys):
        hit = own[k : k + 1, :] == owners
        named = jnp.where(hit, 1.0, named)
        rows = jnp.where(hit, row[k : k + 1, :], rows)
        scales = jnp.where(hit, scale[k : k + 1, :], scales)
    earlier = (iota((batch, batch), 0) < iota((batch, batch), 1)).astype(bf16)
    before = jnp.dot(named.astype(bf16), earlier, preferred_element_type=f32)
    place = jnp.where(named > 0, before + 1.0, 0.0)
    place_ref[...] = place
    scale_ref[...] = scales
    lanes = iota((devices, capacity), 1)
    asks = jnp.zeros((devices, capacity), f32)
    for s in range(capacity):
        col = jnp.sum(jnp.where(place == s + 1.0, rows, 0.0), axis=1, keepdims=True)
        asks = jnp.where(lanes == s, col, asks)
    asks_ref[...] = asks.astype(i32)
    din, rows_hot, width = w_ref.shape[0], hot_ref.shape[0] // 2, hot_ref.shape[1]
    copies[3].wait()
    half_ref[din:, :width] = hot_ref[:rows_hot, :].astype(bf16)
    half_ref[din:, width:] = hot_ref[rows_hot:, :].astype(bf16)
    copies[4].wait()
    half_ref[:din, :] = w_ref[...].astype(bf16)
    for which, axis in ((0, "x"), (1, "z")):
        at = lax.axis_index(axis)
        for first, count, to in ((0, din // 8, 0), (din, rows_hot // 8, din // 8)):
            start = pl.multiple_of(first + which * 4 * count + at * count, count)
            to += which * (din + rows_hot) // 8
            quarter_ref[to : to + count, :] = half_ref[pl.ds(start, count), :]


def route(own, row, expo, hot, w, devices, capacity):
    batch = own.shape[1]
    return pl.pallas_call(
        route_kernel,
        out_shape=(
            jax.ShapeDtypeStruct((devices, capacity), i32),
            jax.ShapeDtypeStruct((devices, batch), f32),
            jax.ShapeDtypeStruct((devices, batch), f32),
            jax.ShapeDtypeStruct((w.shape[0] + hot.shape[0] // 2, w.shape[1]), bf16),
            jax.ShapeDtypeStruct((w.shape[0] // 4 + hot.shape[0] // 8, w.shape[1]), bf16),
        ),
        in_specs=[HBM] * 5,
        out_specs=(VM,) * 5,
        scratch_shapes=[
            pltpu.VMEM(own.shape, i32),
            pltpu.VMEM(row.shape, i32),
            pltpu.VMEM(expo.shape, i32),
            pltpu.VMEM(hot.shape, f32),
            pltpu.VMEM(w.shape, f32),
            pltpu.SemaphoreType.DMA((5,)),
        ],
        compiler_params=ALONE,
        cost_estimate=cost(2),
        name="route",
    )(own, row, expo, hot, w)


def spread_kernel(place_ref, scale_ref, out_hbm, out_ref, sem):
    devices, batch = place_ref.shape
    capacity = out_ref.shape[0] // devices
    full = (devices, capacity, batch)
    slots = (iota(full, 1) + 1).astype(f32)
    place = jnp.broadcast_to(place_ref[...][:, None, :], full)
    scale = jnp.broadcast_to(scale_ref[...][:, None, :], full)
    out = jnp.where(place == slots, scale, 0.0)
    out_ref[...] = out.reshape(devices * capacity, batch).astype(bf16)
    copy = pltpu.make_async_copy(out_ref, out_hbm, sem)
    copy.start()
    copy.wait()


def spread(place, scale, capacity):
    devices, batch = place.shape
    shape = (devices * capacity, batch)
    return pl.pallas_call(
        spread_kernel,
        out_shape=jax.ShapeDtypeStruct(shape, bf16),
        in_specs=[VM] * 2,
        out_specs=HBM,
        scratch_shapes=[pltpu.VMEM(shape, bf16), pltpu.SemaphoreType.DMA],
        compiler_params=ALONE,
        cost_estimate=cost(1),
        name="spread",
    )(place, scale)


def lookup_kernel(asked_ref, table_hbm, out_hbm, table_ref, out_ref, sem, sems):
    devices, capacity = asked_ref.shape
    slots, width = out_ref.shape
    rows = table_ref.shape[0]
    load = pltpu.make_async_copy(table_hbm, table_ref, sem)
    load.start()
    full = (devices, capacity, capacity)
    wide = jnp.broadcast_to(asked_ref[...].astype(f32)[:, None, :], full)
    kept = jnp.where(iota(full, 1) == iota(full, 2), wide, 0.0).reshape(slots, capacity)
    col = jnp.sum(kept, axis=1, keepdims=True).astype(i32)
    load.wait()
    step = 256
    copies = []
    for at in range(0, slots, step):
        hit = col[at : at + step] == iota((step, rows), 1)
        onehot = jnp.where(hit, 1.0, 0.0).astype(bf16)
        got = jnp.dot(onehot, table_ref[...], preferred_element_type=f32)
        out_ref[at : at + step, :] = got.astype(bf16)
        copies.append(
            pltpu.make_async_copy(
                out_ref.at[at : at + step], out_hbm.at[at : at + step], sems.at[at // step]
            )
        )
        copies[-1].start()
    for copy in copies:
        copy.wait()


def lookup(asked, table):
    devices, capacity = asked.shape
    shape = (devices * capacity, table.shape[1])
    return pl.pallas_call(
        lookup_kernel,
        out_shape=jax.ShapeDtypeStruct(shape, bf16),
        in_specs=[VM, HBM],
        out_specs=HBM,
        scratch_shapes=[
            pltpu.VMEM(table.shape, bf16),
            pltpu.VMEM(shape, bf16),
            pltpu.SemaphoreType.DMA,
            pltpu.SemaphoreType.DMA((shape[0] // 256,)),
        ],
        compiler_params=ALONE,
        cost_estimate=cost(3),
        name="lookup",
    )(asked, table)


def contract_rows(a, b):
    return lax.dot_general(a, b, (((0,), (0,)), ((), ())), preferred_element_type=f32)


def gather_copies(refs, first, buf, sems):
    x, z = lax.axis_index("x"), lax.axis_index("z")
    rows = buf.shape[2]
    count = rows // 8
    start = first // 8
    lists = []
    n = 0
    for side in range(2):
        half, *others = refs[9 * side : 9 * side + 9]
        copies = [
            pltpu.make_async_copy(half.at[first : first + rows], buf.at[side, 0], sems.at[n])
        ]
        n += 1
        for which, at in ((0, x), (1, z)):
            for d in range(4):
                to = lax.rem(at + d, 4) * count + which * 4 * count
                to_rows = pl.ds(pl.multiple_of(to, count), count)
                src = others[4 * which + d].at[:, start : start + count]
                dst = buf.at[side, 1:4, to_rows]
                copies.append(pltpu.make_async_copy(src, dst, sems.at[n]))
                n += 1
        lists.append(copies)
    for copies in lists:
        copies[0].start()
    for copies in lists:
        for copy in copies[1:]:
            copy.start()
    return lists


COPIES = 2 * 9


def count_kernel(ids_ref, out_hbm, out_ref, sem):
    batch, keys = ids_ref.shape
    rows = out_ref.shape[1] // 8
    y, core = lax.axis_index("y"), lax.axis_index("core")
    ids = ids_ref[...]
    for t in range(8):
        side = core if t < 4 else 1 - core
        first = (2 * lax.rem(y + t, 4) + side) * rows
        lanes = iota((batch, rows), 1) + first
        counts = jnp.zeros((batch, rows), f32)
        for k in range(keys):
            counts += jnp.where(ids[:, k : k + 1] == lanes, 1.0, 0.0)
        out_ref[:, t * rows : (t + 1) * rows] = counts.astype(bf16)
    copy = pltpu.make_async_copy(out_ref, out_hbm, sem)
    copy.start()
    copy.wait()


def count_of(ids, rows):
    shape = (ids.shape[0], 8 * rows)
    return pl.pallas_call(
        count_kernel,
        out_shape=jax.ShapeDtypeStruct(shape, bf16),
        in_specs=[VM],
        out_specs=HBM,
        scratch_shapes=[pltpu.VMEM(shape, bf16), pltpu.SemaphoreType.DMA],
        compiler_params=ALONE,
        cost_estimate=cost(3),
        name="count",
    )(ids)


def hot_pool_kernel(counts_hbm, *refs):
    refs, (out_ref, buf, counts_ref, sem, sems) = refs[:-5], refs[-5:]
    _, _, rows, wide = buf.shape
    width = out_ref.shape[1]
    early = pltpu.make_async_copy(counts_hbm, counts_ref, sem)
    early.start()
    lists = gather_copies(refs, refs[0].shape[0] - rows, buf, sems)
    early.wait()
    pool = jnp.zeros(out_ref.shape, f32)
    for side, copies in enumerate(lists):
        for copy in copies:
            copy.wait()
        for y in range(4):
            at = (4 * side + y) * 2 * rows
            counts = counts_ref[:, at : at + 2 * rows]
            part = buf[side, y]
            pool += jnp.dot(counts[:, :rows], part[:, :width], preferred_element_type=f32)
            pool += jnp.dot(counts[:, rows:], part[:, width:], preferred_element_type=f32)
    out_ref[...] = pool.astype(bf16)


def hot_pooled(counts, pieces, width):
    wide = pieces[0].shape[1]
    rows = pieces[0].shape[0] - 2 * width
    return pl.pallas_call(
        hot_pool_kernel,
        out_shape=jax.ShapeDtypeStruct((counts.shape[0], width), bf16),
        in_specs=[HBM] * (1 + len(pieces)),
        out_specs=VM,
        scratch_shapes=[
            pltpu.VMEM((2, 4, rows, wide), bf16),
            pltpu.VMEM(counts.shape, bf16),
            pltpu.SemaphoreType.DMA,
            pltpu.SemaphoreType.DMA((COPIES,)),
        ],
        compiler_params=ALONE,
        cost_estimate=cost(0.1),
        name="hot_pool",
    )(counts, *pieces)


def tower_kernel(hot_ref, head_ref, label_ref, ids_ref, returned_ref, spread_hbm, *refs):
    pieces, refs = refs[:-9], refs[-9:]
    out_hbm, load_ref, pre_ref, sig_ref, spread_ref, w_ref, out_ref, two, sems = refs
    batch, width = hot_ref.shape
    _, _, din, part = w_ref.shape
    parts = 8
    keys = ids_ref.shape[1]
    early = pltpu.make_async_copy(spread_hbm, spread_ref, two.at[0])
    early.start()
    lists = gather_copies(pieces, 0, w_ref, sems)
    early.wait()
    cold = contract_rows(spread_ref[...], returned_ref[...]).astype(bf16)
    feat = jnp.concatenate([hot_ref[...], cold], axis=1)
    logit = jnp.zeros((batch, 1), f32)
    waits = {0: lists[0][:1], 4: lists[1][:1], 1: lists[0][1:], 5: lists[1][1:]}
    for t in (0, 4, 1, 2, 3, 5, 6, 7):
        cols = slice(t * part, (t + 1) * part)
        for copy in waits.get(t, ()):
            copy.wait()
        pre = jnp.dot(feat, w_ref[t // 4, t % 4], preferred_element_type=f32)
        sig = jax.nn.sigmoid(pre)
        pre_ref[:, cols] = pre
        sig_ref[:, cols] = sig
        logit += jnp.sum(pre * sig * head_ref[:, cols], axis=1, keepdims=True)
    dlogit = jax.nn.sigmoid(logit) - label_ref[...]
    dfeat = jnp.zeros((batch, din), f32)
    for t in range(parts):
        cols = slice(t * part, (t + 1) * part)
        pre = pre_ref[:, cols]
        sig = sig_ref[:, cols]
        dpre = (dlogit * head_ref[:, cols] * sig * (1.0 + pre * (1.0 - sig))).astype(bf16)
        dfeat += lax.dot_general(
            dpre, w_ref[t // 4, t % 4], (((1,), (1,)), ((), ())), preferred_element_type=f32
        )
    dhot = dfeat[:, :width]
    dcold = dfeat[:, width:].astype(bf16)
    out_ref[...] = jnp.dot(spread_ref[...], dcold, preferred_element_type=f32).astype(bf16)
    last = pltpu.make_async_copy(out_ref, out_hbm, two.at[1])
    last.start()
    load_ref[:, :din] = feat
    load_ref[:, din : din + width] = dhot.astype(bf16)
    first = dlogit.astype(bf16).astype(f32)
    second = (dlogit - first).astype(bf16).astype(f32)
    third = dlogit - first - second
    lanes = iota((batch, 128), 1)
    extra = jnp.where(lanes == 0, first, 0.0)
    extra = jnp.where(lanes == 1, second, extra)
    extra = jnp.where(lanes == 2, third, extra)
    ids = ids_ref[...]
    high = lax.shift_right_logical(ids, 6)
    low = ids - high * 64
    high = high.astype(f32)
    low = low.astype(f32)
    for k in range(keys):
        extra = jnp.where(lanes == 8 + k, high[:, k : k + 1], extra)
        extra = jnp.where(lanes == 8 + keys + k, low[:, k : k + 1], extra)
    load_ref[:, din + width :] = extra.astype(bf16)
    last.wait()


def tower(hot, returned, spread_mat, head, label, ids, pieces):
    batch, width = hot.shape
    hidden = head.shape[1]
    return pl.pallas_call(
        tower_kernel,
        out_shape=(
            jax.ShapeDtypeStruct(returned.shape, bf16),
            jax.ShapeDtypeStruct((batch, 3 * width + 128), bf16),
        ),
        in_specs=[VM] * 5 + [HBM] * (1 + len(pieces)),
        out_specs=(HBM, VM),
        scratch_shapes=[
            pltpu.VMEM((batch, hidden), f32),
            pltpu.VMEM((batch, hidden), f32),
            pltpu.VMEM(spread_mat.shape, bf16),
            pltpu.VMEM((2, 4, 2 * width, hidden // 8), bf16),
            pltpu.VMEM(returned.shape, bf16),
            pltpu.SemaphoreType.DMA((2,)),
            pltpu.SemaphoreType.DMA((COPIES,)),
        ],
        compiler_params=MOST,
        cost_estimate=cost(6),
        name="tower",
    )(hot, head, label, ids, returned, spread_mat, *pieces)


def hold_kernel(in_ref, out_ref):
    pass


def hold(value):
    return pl.pallas_call(
        hold_kernel,
        out_shape=jax.ShapeDtypeStruct(value.shape, value.dtype),
        in_specs=[HBM],
        out_specs=HBM,
        input_output_aliases={0: 0},
        compiler_params=ALONE,
        cost_estimate=cost(30),
        name="hold",
    )(value)


def columns_kernel(keys, last, head_ref, half_hbm, *refs):
    if last:
        before_hbm, *refs = refs
        *loads, out_ref, half_ref, load_ref, sems, before_ref = refs
    else:
        *loads, out_ref, half_ref, load_ref, sems = refs
    din, part = half_ref.shape
    rows, width = din, din // 2
    batch = loads[0].shape[0]
    count = len(loads)
    first = pltpu.make_async_copy(half_hbm.at[:din], half_ref, sems.at[count])
    first.start()
    copies = [
        pltpu.make_async_copy(ref, load_ref.at[pl.ds(n * batch, batch)], sems.at[n])
        for n, ref in enumerate(loads)
    ]
    for copy in copies:
        copy.start()
    if last:
        before = pltpu.make_async_copy(before_hbm, before_ref, sems.at[count + 1])
        before.start()
    first.wait()
    base = (2 * lax.axis_index("y") + lax.axis_index("core")) * rows
    lanes = (iota((2 * batch, rows), 1) + base).astype(f32)
    tower_grad = jnp.zeros((din, part), f32)
    hot_grad = jnp.zeros((rows, width), f32)
    for n in range(0, count, 2):
        copies[n].wait()
        copies[n + 1].wait()
        at = slice(n * batch, (n + 2) * batch)
        feat = load_ref[at, :din]
        extra = load_ref[at, din + width :].astype(f32)
        dlogit = extra[:, 0:1] + extra[:, 1:2] + extra[:, 2:3]
        pre = jnp.dot(feat, half_ref[...], preferred_element_type=f32)
        sig = jax.nn.sigmoid(pre)
        dpre = (dlogit * head_ref[...] * sig * (1.0 + pre * (1.0 - sig))).astype(bf16)
        tower_grad += contract_rows(feat, dpre)
        counts = jnp.zeros((2 * batch, rows), f32)
        for k in range(keys):
            ids = extra[:, 8 + k : 9 + k] * 64.0 + extra[:, 8 + keys + k : 9 + keys + k]
            counts += jnp.where(ids == lanes, 1.0, 0.0)
        hot_grad += contract_rows(counts.astype(bf16), load_ref[at, din : din + width])
    if last:
        before.wait()
        out_ref[:, :part] = (tower_grad + before_ref[:, :part]).astype(bf16)
        out_ref[:, part:] = (hot_grad + before_ref[:, part:]).astype(bf16)
    else:
        out_ref[:, :part] = tower_grad
        out_ref[:, part:] = hot_grad


def columns(loads, half, head, keys, before=()):
    batch, wide = loads[0].shape
    rows, part = half.shape[1], head.shape[1]
    shape = (rows, half.shape[0])
    last = len(before) > 0
    return pl.pallas_call(
        functools.partial(columns_kernel, keys, last),
        out_shape=jax.ShapeDtypeStruct(shape, bf16 if last else f32),
        in_specs=[VM] + [HBM] * (1 + len(before) + len(loads)),
        out_specs=VM,
        scratch_shapes=[
            pltpu.VMEM((rows, part), bf16),
            pltpu.VMEM((batch * len(loads), wide), bf16),
            pltpu.SemaphoreType.DMA((2 + len(loads),)),
        ]
        + [pltpu.VMEM(shape, f32)] * len(before),
        compiler_params=ALONE,
        cost_estimate=cost(0.2),
        name="columns",
    )(head, half, *before, *loads)


def total_kernel(terms_ref, left_ref, right_ref):
    total = terms_ref[0].astype(f32)
    for n in range(1, terms_ref.shape[0]):
        total += terms_ref[n].astype(f32)
    half = left_ref.shape[1]
    left_ref[...] = total[:, :half]
    right_ref[...] = total[:, half:]


def total_of(terms):
    _, rows, wide = terms.shape
    return pl.pallas_call(
        total_kernel,
        out_shape=(jax.ShapeDtypeStruct((rows, wide // 2), f32),) * 2,
        in_specs=[VM],
        out_specs=(VM,) * 2,
        compiler_params=PARAMS,
        cost_estimate=cost(1),
        name="total",
    )(terms)


def lay_kernel(*refs):
    out0, out1 = refs[-2:]
    for axis, parts, out in (("z", refs[:4], out0), ("x", refs[4:8], out1)):
        step = parts[0].shape[0]
        for n, ref in enumerate(parts):
            at = lax.rem(lax.axis_index(axis) + n, 4) * step
            out[pl.ds(pl.multiple_of(at, step), step), :] = ref[...]


def lay(left, right):
    rows, wide = left[0].shape
    return pl.pallas_call(
        lay_kernel,
        out_shape=(jax.ShapeDtypeStruct((4 * rows, wide), f32),) * 2,
        in_specs=[VM] * 8,
        out_specs=(VM,) * 2,
        compiler_params=PARAMS,
        cost_estimate=cost(1),
        name="lay",
    )(*left, *right)


def update_kernel(l0, l1, l2, l3, r0, r1, r2, r3, *refs):
    w_ref, w_acc_ref, hot_ref, hot_acc_ref, nw_ref, nwa_ref, nh_ref, nha_ref, grad_ref = refs
    part = w_ref.shape[1]
    step, half = l0.shape
    piece = step // 4
    i = pl.program_id(0)
    for d, left in enumerate((l0, l1, l2, l3)):

        @pl.when(lax.rem(lax.axis_index("x") + d, 4) == i)
        def _():
            grad_ref[:, :half] = left[...]

    start = pl.multiple_of(i * piece, piece)
    for d, right in enumerate((r0, r1, r2, r3)):
        at = lax.rem(lax.axis_index("z") + d, 4) * piece
        grad_ref[pl.ds(pl.multiple_of(at, piece), piece), half:] = right[pl.ds(start, piece), :]
    nw, nwa = adagrad(w_ref[...], w_acc_ref[...], grad_ref[:, :part])
    nw_ref[...] = nw
    nwa_ref[...] = nwa
    nh, nha = adagrad(hot_ref[...], hot_acc_ref[...], grad_ref[:, part:])
    nh_ref[...] = nh
    nha_ref[...] = nha


def update(left, right, w, w_acc, hot, hot_acc):
    step, half = left[0].shape
    w_block = pl.BlockSpec((step, w.shape[1]), lambda i: (i, 0))
    hot_block = pl.BlockSpec((step, hot.shape[1]), lambda i: (i, 0))
    return pl.pallas_call(
        update_kernel,
        grid=(4,),
        in_specs=[VM] * 8
        + [w_block] * 2
        + [hot_block] * 2,
        out_specs=(w_block, w_block, hot_block, hot_block),
        out_shape=(jax.ShapeDtypeStruct(w.shape, f32),) * 2
        + (jax.ShapeDtypeStruct(hot.shape, f32),) * 2,
        scratch_shapes=[pltpu.VMEM((step, 2 * half), f32)],
        compiler_params=PARAMS,
        cost_estimate=cost(4),
        name="update",
    )(*left, *right, w, w_acc, hot, hot_acc)


def stage_kernel(*refs):
    count = len(refs) // 2
    sems = refs[-1]
    copies = [
        pltpu.make_async_copy(refs[n], refs[count + n], sems.at[n]) for n in range(count)
    ]
    for copy in copies:
        copy.start()
    for copy in copies:
        copy.wait()


def stage(values):
    return pl.pallas_call(
        stage_kernel,
        out_shape=tuple(jax.ShapeDtypeStruct(value.shape, value.dtype) for value in values),
        in_specs=[HBM] * len(values),
        out_specs=(VM,) * len(values),
        scratch_shapes=[pltpu.SemaphoreType.DMA((len(values),))],
        compiler_params=PARAMS,
        cost_estimate=cost(4),
        name="stage",
    )(*values)


def cold_kernel(asked_ref, grads_ref, table_ref, acc_ref, new_ref, new_acc_ref):
    step, width = table_ref.shape
    slots = grads_ref.shape[0]
    rows = iota((step, slots), 0) + pl.program_id(0) * step
    onehot = jnp.where(asked_ref[...] == rows, 1.0, 0.0).astype(bf16)
    grad = jnp.dot(onehot, grads_ref[...], preferred_element_type=f32)
    param, acc = adagrad(table_ref[...], acc_ref[...], grad)
    new_ref[...] = param
    new_acc_ref[...] = acc


def cold_update(asked, grads, table, acc):
    rows, width = table.shape
    slots = grads.shape[0]
    step = 256
    block = pl.BlockSpec((step, width), lambda i: (i, 0))
    return pl.pallas_call(
        cold_kernel,
        grid=(rows // step,),
        out_shape=(jax.ShapeDtypeStruct(table.shape, f32),) * 2,
        in_specs=[
            pl.BlockSpec((1, slots), lambda i: (0, 0)),
            pl.BlockSpec((slots, width), lambda i: (0, 0)),
            block,
            block,
        ],
        out_specs=(block, block),
        compiler_params=PARAMS,
        cost_estimate=cost(5),
        name="cold_update",
    )(asked, grads, table, acc)


def along(value, axis, by):
    return lax.ppermute(value, axis, [((i + by) % 4, i) for i in range(4)])


def around(value, axis):
    last, one = along(value, axis, 3), along(value, axis, 1)
    return value, one, along(value, axis, 2), last


def swap(value):
    return lax.ppermute(value, "core", [(0, 1), (1, 0)])


def on_device(
    hot_ids,
    cold_owner,
    cold_row,
    cold_exp,
    labels,
    head_w,
    hot_table,
    hot_acc,
    cold_table,
    cold_acc,
    tower_w,
    tower_acc,
):
    devices = math.prod(lax.axis_size(name) for name in ALL)
    y, core = lax.axis_index("y"), lax.axis_index("core")
    me = 2 * y + core
    batch, keys = hot_ids.shape
    hot_rows, width = hot_table.shape
    part = tower_w.shape[1]
    capacity = max(2, 2 * batch * cold_owner.shape[1] // devices)
    asks, place, scale, half, quarter = route(
        cold_owner.T, cold_row.T, cold_exp.T, hot_table, tower_w, devices, capacity
    )
    asked = lax.all_to_all(asks, ALL, split_axis=0, concat_axis=0, tiled=True)
    spread_mat = spread(place, scale, capacity)
    quarters = tuple(along(quarter, "y", by) for by in (1, 2, 3))
    counts = count_of(hot_ids, hot_rows)
    cold_half = cold_table.astype(bf16)
    asked, counts, cold_half, spread_mat = lax.optimization_barrier(
        (asked, counts, cold_half, spread_mat)
    )
    count = quarter.shape[0] // 2
    by_x = jnp.stack([value[:count] for value in quarters])
    by_z = jnp.stack([value[count:] for value in quarters])
    looked = lookup(asked, cold_half)
    xs = tuple(along(by_x, "x", by) for by in (1, 2, 3))
    zs = tuple(along(by_z, "z", by) for by in (1, 2, 3))
    returned = lax.all_to_all(
        looked.reshape(devices, capacity, width), ALL, split_axis=0, concat_axis=0, tiled=True
    ).reshape(-1, width)
    pieces = lax.optimization_barrier((half, by_x) + xs + (by_z,) + zs)
    pieces += tuple(swap(value) for value in pieces)
    hot_feat = hot_pooled(counts, pieces, width)
    heads = head_w.reshape(4, 2, part)
    turned = jnp.concatenate([heads, heads])
    turned = lax.dynamic_slice_in_dim(turned, y, 4, 0)
    head = jnp.concatenate(
        [lax.dynamic_slice_in_dim(turned, side, 1, 1).reshape(1, -1) for side in (core, 1 - core)],
        axis=1,
    )
    outgoing, load = tower(
        hot_feat, returned, spread_mat, head, labels[:, None], hot_ids, pieces
    )
    loads = around(load, "y")
    outgoing, loads = lax.optimization_barrier((outgoing, loads))
    incoming = lax.all_to_all(
        outgoing.reshape(devices, capacity, width), ALL, split_axis=0, concat_axis=0, tiled=True
    ).reshape(-1, width)
    loads += tuple(swap(part) for part in loads)
    head_part = lax.dynamic_slice(head_w, (me * part,), (part,))[None, :]
    own, one, two, last = loads[:4]
    early = columns((own, loads[4], one, last), half, head_part, keys)
    partial = columns((two,) + loads[5:], half, head_part, keys, (early,))
    partial, incoming = lax.optimization_barrier((partial, incoming))
    terms = lax.all_to_all(partial, ("x", "z"), split_axis=0, concat_axis=0, tiled=True)
    new_cold = cold_update(asked.reshape(1, -1), incoming, cold_table, cold_acc)
    terms, (new_cold, new_cold_acc) = lax.optimization_barrier((terms, new_cold))
    left, right = total_of(terms.reshape(16, -1, part + width))
    left, right = lay(around(left, "z"), around(right, "x"))
    params = (tower_w, tower_acc, hot_table, hot_acc)
    left, right, params = lax.optimization_barrier((left, right, params))
    params = stage(params)
    left, right = around(left, "x"), around(right, "z")
    new_w, new_w_acc, new_hot, new_hot_acc = update(
        left, right, *params
    )
    return (new_hot, new_hot_acc, new_cold, new_cold_acc, new_w, new_w_acc)


def solution(mesh):
    chips = mesh.devices.reshape(4, 2, 4, 4)
    mesh = jax.sharding.Mesh(chips, ALL)
    split = P(ALL, None)
    rows = P(TABLE, None)
    cols = P(None, TABLE)
    return jax.shard_map(
        on_device,
        mesh=mesh,
        in_specs=(split,) * 4 + (P(ALL), P(), rows, rows, split, split, cols, cols),
        out_specs=(rows, rows, split, split, cols, cols),
        check_vma=False,
    )
```

```python
import functools
import math

import jax
import jax.numpy as jnp
from jax import lax
from jax.experimental import pallas as pl
from jax.experimental.pallas import tpu as pltpu
from jax.sharding import PartitionSpec as P

learn_rate = 0.05
bf16 = jnp.bfloat16
f32 = jnp.float32
i32 = jnp.int32
ALL = ("y", "core", "z", "x")
TABLE = ("y", "core")
VM = pl.BlockSpec(memory_space=pltpu.VMEM)
HBM = pl.BlockSpec(memory_space=pltpu.HBM)
MIB = 1024 * 1024
PARAMS = pltpu.CompilerParams(vmem_limit_bytes=24 * MIB)
MOST = pltpu.CompilerParams(vmem_limit_bytes=57 * MIB)
ALONE = pltpu.CompilerParams(vmem_limit_bytes=60 * MIB)


def adagrad(param, accum, grad):
    new_accum = accum + grad * grad
    return (param - learn_rate * grad * lax.rsqrt(new_accum), new_accum)


def cost(us):
    return pl.CostEstimate(flops=int(us * 1e9), bytes_accessed=int(us * 3e6), transcendentals=0)


def iota(shape, axis):
    return lax.broadcasted_iota(i32, shape, axis)


def route_kernel(
    own_hbm,
    row_hbm,
    exp_hbm,
    hot_hbm,
    w_hbm,
    asks_ref,
    place_ref,
    scale_ref,
    half_ref,
    quarter_ref,
    own_ref,
    row_ref,
    exp_ref,
    hot_ref,
    w_ref,
    sems,
):
    pairs = (
        (own_hbm, own_ref),
        (row_hbm, row_ref),
        (exp_hbm, exp_ref),
        (hot_hbm, hot_ref),
        (w_hbm, w_ref),
    )
    copies = [pltpu.make_async_copy(a, b, sems.at[n]) for n, (a, b) in enumerate(pairs)]
    for copy in copies:
        copy.start()
    for copy in copies[:3]:
        copy.wait()
    keys, batch = own_ref.shape
    devices, capacity = asks_ref.shape
    owners = iota((devices, batch), 0)
    named = jnp.zeros((devices, batch), f32)
    rows = jnp.zeros((devices, batch), f32)
    scales = jnp.zeros((devices, batch), f32)
    expo = exp_ref[...]
    scale = jnp.where(expo == 0, 1.0, jnp.where(expo == 1, 0.5, 0.25))
    row = row_ref[...].astype(f32)
    own = own_ref[...]
    for k in range(keys):
        hit = own[k : k + 1, :] == owners
        named = jnp.where(hit, 1.0, named)
        rows = jnp.where(hit, row[k : k + 1, :], rows)
        scales = jnp.where(hit, scale[k : k + 1, :], scales)
    earlier = (iota((batch, batch), 0) < iota((batch, batch), 1)).astype(bf16)
    before = jnp.dot(named.astype(bf16), earlier, preferred_element_type=f32)
    place = jnp.where(named > 0, before + 1.0, 0.0)
    place_ref[...] = place
    scale_ref[...] = scales
    lanes = iota((devices, capacity), 1)
    asks = jnp.zeros((devices, capacity), f32)
    for s in range(capacity):
        col = jnp.sum(jnp.where(place == s + 1.0, rows, 0.0), axis=1, keepdims=True)
        asks = jnp.where(lanes == s, col, asks)
    asks_ref[...] = asks.astype(i32)
    din, rows_hot, width = w_ref.shape[0], hot_ref.shape[0] // 2, hot_ref.shape[1]
    copies[3].wait()
    half_ref[din:, :width] = hot_ref[:rows_hot, :].astype(bf16)
    half_ref[din:, width:] = hot_ref[rows_hot:, :].astype(bf16)
    copies[4].wait()
    half_ref[:din, :] = w_ref[...].astype(bf16)
    for which, axis in ((0, "x"), (1, "z")):
        at = lax.axis_index(axis)
        for first, count, to in ((0, din // 8, 0), (din, rows_hot // 8, din // 8)):
            start = pl.multiple_of(first + which * 4 * count + at * count, count)
            to += which * (din + rows_hot) // 8
            quarter_ref[to : to + count, :] = half_ref[pl.ds(start, count), :]


def route(own, row, expo, hot, w, devices, capacity):
    batch = own.shape[1]
    return pl.pallas_call(
        route_kernel,
        out_shape=(
            jax.ShapeDtypeStruct((devices, capacity), i32),
            jax.ShapeDtypeStruct((devices, batch), f32),
            jax.ShapeDtypeStruct((devices, batch), f32),
            jax.ShapeDtypeStruct((w.shape[0] + hot.shape[0] // 2, w.shape[1]), bf16),
            jax.ShapeDtypeStruct((w.shape[0] // 4 + hot.shape[0] // 8, w.shape[1]), bf16),
        ),
        in_specs=[HBM] * 5,
        out_specs=(VM,) * 5,
        scratch_shapes=[
            pltpu.VMEM(own.shape, i32),
            pltpu.VMEM(row.shape, i32),
            pltpu.VMEM(expo.shape, i32),
            pltpu.VMEM(hot.shape, f32),
            pltpu.VMEM(w.shape, f32),
            pltpu.SemaphoreType.DMA((5,)),
        ],
        compiler_params=ALONE,
        cost_estimate=cost(2),
        name="route",
    )(own, row, expo, hot, w)


def spread_kernel(place_ref, scale_ref, out_hbm, out_ref, sem):
    devices, batch = place_ref.shape
    capacity = out_ref.shape[0] // devices
    full = (devices, capacity, batch)
    slots = (iota(full, 1) + 1).astype(f32)
    place = jnp.broadcast_to(place_ref[...][:, None, :], full)
    scale = jnp.broadcast_to(scale_ref[...][:, None, :], full)
    out = jnp.where(place == slots, scale, 0.0)
    out_ref[...] = out.reshape(devices * capacity, batch).astype(bf16)
    copy = pltpu.make_async_copy(out_ref, out_hbm, sem)
    copy.start()
    copy.wait()


def spread(place, scale, capacity):
    devices, batch = place.shape
    shape = (devices * capacity, batch)
    return pl.pallas_call(
        spread_kernel,
        out_shape=jax.ShapeDtypeStruct(shape, bf16),
        in_specs=[VM] * 2,
        out_specs=HBM,
        scratch_shapes=[pltpu.VMEM(shape, bf16), pltpu.SemaphoreType.DMA],
        compiler_params=ALONE,
        cost_estimate=cost(1),
        name="spread",
    )(place, scale)


def lookup_kernel(asked_hbm, table_hbm, out_hbm, asked_ref, table_ref, out_ref, two, sems):
    devices, capacity = asked_ref.shape
    slots, width = out_ref.shape
    rows = table_ref.shape[0]
    first = pltpu.make_async_copy(asked_hbm, asked_ref, two.at[0])
    load = pltpu.make_async_copy(table_hbm, table_ref, two.at[1])
    first.start()
    load.start()
    first.wait()
    full = (devices, capacity, capacity)
    wide = jnp.broadcast_to(asked_ref[...].astype(f32)[:, None, :], full)
    kept = jnp.where(iota(full, 1) == iota(full, 2), wide, 0.0).reshape(slots, capacity)
    col = jnp.sum(kept, axis=1, keepdims=True).astype(i32)
    load.wait()
    step = 256
    copies = []
    for at in range(0, slots, step):
        hit = col[at : at + step] == iota((step, rows), 1)
        onehot = jnp.where(hit, 1.0, 0.0).astype(bf16)
        got = jnp.dot(onehot, table_ref[...], preferred_element_type=f32)
        out_ref[at : at + step, :] = got.astype(bf16)
        copies.append(
            pltpu.make_async_copy(
                out_ref.at[at : at + step], out_hbm.at[at : at + step], sems.at[at // step]
            )
        )
        copies[-1].start()
    for copy in copies:
        copy.wait()


def lookup(asked, table):
    devices, capacity = asked.shape
    shape = (devices * capacity, table.shape[1])
    return pl.pallas_call(
        lookup_kernel,
        out_shape=jax.ShapeDtypeStruct(shape, bf16),
        in_specs=[HBM, HBM],
        out_specs=HBM,
        scratch_shapes=[
            pltpu.VMEM(asked.shape, i32),
            pltpu.VMEM(table.shape, bf16),
            pltpu.VMEM(shape, bf16),
            pltpu.SemaphoreType.DMA((2,)),
            pltpu.SemaphoreType.DMA((shape[0] // 256,)),
        ],
        compiler_params=ALONE,
        cost_estimate=cost(3),
        name="lookup",
    )(asked, table)


def contract_rows(a, b):
    return lax.dot_general(a, b, (((0,), (0,)), ((), ())), preferred_element_type=f32)


def gather_copies(refs, first, buf, sems):
    x, z = lax.axis_index("x"), lax.axis_index("z")
    rows = buf.shape[2]
    count = rows // 8
    start = first // 8
    lists = []
    n = 0
    for side in range(2):
        half, *others = refs[9 * side : 9 * side + 9]
        copies = [
            pltpu.make_async_copy(half.at[first : first + rows], buf.at[side, 0], sems.at[n])
        ]
        n += 1
        for which, at in ((0, x), (1, z)):
            for d in range(4):
                to = lax.rem(at + d, 4) * count + which * 4 * count
                to_rows = pl.ds(pl.multiple_of(to, count), count)
                src = others[4 * which + d].at[:, start : start + count]
                dst = buf.at[side, 1:4, to_rows]
                copies.append(pltpu.make_async_copy(src, dst, sems.at[n]))
                n += 1
        lists.append(copies)
    for n, copies in enumerate(lists):
        copies[0].start(priority=n)
    for copies in lists:
        for n, copy in enumerate(copies[1:]):
            copy.start(priority=n % 2)
    return lists


COPIES = 2 * 9


def count_kernel(ids_ref, out_hbm, out_ref, sem):
    batch, keys = ids_ref.shape
    rows = out_ref.shape[1] // 8
    y, core = lax.axis_index("y"), lax.axis_index("core")
    ids = ids_ref[...]
    for t in range(8):
        side = core if t < 4 else 1 - core
        first = (2 * lax.rem(y + t, 4) + side) * rows
        lanes = iota((batch, rows), 1) + first
        counts = jnp.zeros((batch, rows), f32)
        for k in range(keys):
            counts += jnp.where(ids[:, k : k + 1] == lanes, 1.0, 0.0)
        out_ref[:, t * rows : (t + 1) * rows] = counts.astype(bf16)
    copy = pltpu.make_async_copy(out_ref, out_hbm, sem)
    copy.start()
    copy.wait()


def count_of(ids, rows):
    shape = (ids.shape[0], 8 * rows)
    return pl.pallas_call(
        count_kernel,
        out_shape=jax.ShapeDtypeStruct(shape, bf16),
        in_specs=[VM],
        out_specs=HBM,
        scratch_shapes=[pltpu.VMEM(shape, bf16), pltpu.SemaphoreType.DMA],
        compiler_params=ALONE,
        cost_estimate=cost(3),
        name="count",
    )(ids)


def hot_pool_kernel(counts_hbm, *refs):
    refs, (out_ref, buf, counts_ref, sem, sems) = refs[:-5], refs[-5:]
    _, _, rows, wide = buf.shape
    width = out_ref.shape[1]
    early = pltpu.make_async_copy(counts_hbm, counts_ref, sem)
    early.start()
    lists = gather_copies(refs, refs[0].shape[0] - rows, buf, sems)
    early.wait()
    pool = jnp.zeros(out_ref.shape, f32)
    for side, copies in enumerate(lists):
        for copy in copies:
            copy.wait()
        for y in range(4):
            at = (4 * side + y) * 2 * rows
            counts = counts_ref[:, at : at + 2 * rows]
            part = buf[side, y]
            pool += jnp.dot(counts[:, :rows], part[:, :width], preferred_element_type=f32)
            pool += jnp.dot(counts[:, rows:], part[:, width:], preferred_element_type=f32)
    out_ref[...] = pool.astype(bf16)


def hot_pooled(counts, pieces, width):
    wide = pieces[0].shape[1]
    rows = pieces[0].shape[0] - 2 * width
    return pl.pallas_call(
        hot_pool_kernel,
        out_shape=jax.ShapeDtypeStruct((counts.shape[0], width), bf16),
        in_specs=[HBM] * (1 + len(pieces)),
        out_specs=VM,
        scratch_shapes=[
            pltpu.VMEM((2, 4, rows, wide), bf16),
            pltpu.VMEM(counts.shape, bf16),
            pltpu.SemaphoreType.DMA,
            pltpu.SemaphoreType.DMA((COPIES,)),
        ],
        compiler_params=ALONE,
        cost_estimate=cost(0.1),
        name="hot_pool",
    )(counts, *pieces)


def tower_kernel(*refs):
    smalls, pieces, refs = refs[:6], refs[6:-14], refs[-14:]
    out_hbm, load_ref, pre_ref, sig_ref, *held, w_ref, out_ref, two, sems = refs
    small_copies = [
        pltpu.make_async_copy(a, b, two.at[n]) for n, (a, b) in enumerate(zip(smalls, held))
    ]
    for copy in small_copies:
        copy.start()
    hot_ref, returned_ref, spread_ref, head_ref, label_ref, ids_ref = held
    batch, width = hot_ref.shape
    _, _, din, part = w_ref.shape
    parts = 8
    keys = ids_ref.shape[1]
    lists = gather_copies(pieces, 0, w_ref, sems)
    for copy in small_copies:
        copy.wait()
    cold = contract_rows(spread_ref[...], returned_ref[...]).astype(bf16)
    feat = jnp.concatenate([hot_ref[...], cold], axis=1)
    logit = jnp.zeros((batch, 1), f32)
    waits = {0: lists[0][:1], 4: lists[1][:1], 1: lists[0][1:], 5: lists[1][1:]}
    for t in (0, 4, 1, 2, 3, 5, 6, 7):
        cols = slice(t * part, (t + 1) * part)
        for copy in waits.get(t, ()):
            copy.wait()
        pre = jnp.dot(feat, w_ref[t // 4, t % 4], preferred_element_type=f32)
        sig = jax.nn.sigmoid(pre)
        pre_ref[:, cols] = pre
        sig_ref[:, cols] = sig
        logit += jnp.sum(pre * sig * head_ref[:, cols], axis=1, keepdims=True)
    dlogit = jax.nn.sigmoid(logit) - label_ref[...]
    dfeat = jnp.zeros((batch, din), f32)
    for t in range(parts):
        cols = slice(t * part, (t + 1) * part)
        pre = pre_ref[:, cols]
        sig = sig_ref[:, cols]
        dpre = (dlogit * head_ref[:, cols] * sig * (1.0 + pre * (1.0 - sig))).astype(bf16)
        dfeat += lax.dot_general(
            dpre, w_ref[t // 4, t % 4], (((1,), (1,)), ((), ())), preferred_element_type=f32
        )
    dhot = dfeat[:, :width]
    dcold = dfeat[:, width:].astype(bf16)
    out_ref[...] = jnp.dot(spread_ref[...], dcold, preferred_element_type=f32).astype(bf16)
    last = pltpu.make_async_copy(out_ref, out_hbm, two.at[6])
    last.start()
    load_ref[:, :din] = feat
    load_ref[:, din : din + width] = dhot.astype(bf16)
    first = dlogit.astype(bf16).astype(f32)
    second = (dlogit - first).astype(bf16).astype(f32)
    third = dlogit - first - second
    lanes = iota((batch, 128), 1)
    extra = jnp.where(lanes == 0, first, 0.0)
    extra = jnp.where(lanes == 1, second, extra)
    extra = jnp.where(lanes == 2, third, extra)
    ids = ids_ref[...]
    high = lax.shift_right_logical(ids, 6)
    low = ids - high * 64
    high = high.astype(f32)
    low = low.astype(f32)
    for k in range(keys):
        extra = jnp.where(lanes == 8 + k, high[:, k : k + 1], extra)
        extra = jnp.where(lanes == 8 + keys + k, low[:, k : k + 1], extra)
    load_ref[:, din + width :] = extra.astype(bf16)
    last.wait()


def tower(hot, returned, spread_mat, head, label, ids, pieces):
    batch, width = hot.shape
    hidden = head.shape[1]
    smalls = (hot, returned, spread_mat, head, label, ids)
    return pl.pallas_call(
        tower_kernel,
        out_shape=(
            jax.ShapeDtypeStruct(returned.shape, bf16),
            jax.ShapeDtypeStruct((batch, 3 * width + 128), bf16),
        ),
        in_specs=[HBM] * (6 + len(pieces)),
        out_specs=(HBM, VM),
        scratch_shapes=[
            pltpu.VMEM((batch, hidden), f32),
            pltpu.VMEM((batch, hidden), f32),
        ]
        + [pltpu.VMEM(value.shape, value.dtype) for value in smalls]
        + [
            pltpu.VMEM((2, 4, 2 * width, hidden // 8), bf16),
            pltpu.VMEM(returned.shape, bf16),
            pltpu.SemaphoreType.DMA((7,)),
            pltpu.SemaphoreType.DMA((COPIES,)),
        ],
        compiler_params=MOST,
        cost_estimate=cost(6),
        name="tower",
    )(*smalls, *pieces)


def hold_kernel(in_ref, out_ref):
    pass


def hold(value):
    return pl.pallas_call(
        hold_kernel,
        out_shape=jax.ShapeDtypeStruct(value.shape, value.dtype),
        in_specs=[HBM],
        out_specs=HBM,
        input_output_aliases={0: 0},
        compiler_params=ALONE,
        cost_estimate=cost(30),
        name="hold",
    )(value)


def columns_kernel(keys, last, head_ref, half_hbm, *refs):
    if last:
        before_hbm, *refs = refs
        *loads, out_ref, half_ref, load_ref, sems, before_ref = refs
    else:
        *loads, out_ref, half_ref, load_ref, sems = refs
    din, part = half_ref.shape
    rows, width = din, din // 2
    batch = loads[0].shape[0]
    count = len(loads)
    first = pltpu.make_async_copy(half_hbm.at[:din], half_ref, sems.at[count])
    first.start()
    copies = [
        pltpu.make_async_copy(ref, load_ref.at[pl.ds(n * batch, batch)], sems.at[n])
        for n, ref in enumerate(loads)
    ]
    for copy in copies:
        copy.start()
    if last:
        before = pltpu.make_async_copy(before_hbm, before_ref, sems.at[count + 1])
        before.start()
    first.wait()
    base = (2 * lax.axis_index("y") + lax.axis_index("core")) * rows
    lanes = (iota((2 * batch, rows), 1) + base).astype(f32)
    tower_grad = jnp.zeros((din, part), f32)
    hot_grad = jnp.zeros((rows, width), f32)
    for n in range(0, count, 2):
        copies[n].wait()
        copies[n + 1].wait()
        at = slice(n * batch, (n + 2) * batch)
        feat = load_ref[at, :din]
        extra = load_ref[at, din + width :].astype(f32)
        dlogit = extra[:, 0:1] + extra[:, 1:2] + extra[:, 2:3]
        pre = jnp.dot(feat, half_ref[...], preferred_element_type=f32)
        sig = jax.nn.sigmoid(pre)
        dpre = (dlogit * head_ref[...] * sig * (1.0 + pre * (1.0 - sig))).astype(bf16)
        tower_grad += contract_rows(feat, dpre)
        counts = jnp.zeros((2 * batch, rows), f32)
        for k in range(keys):
            ids = extra[:, 8 + k : 9 + k] * 64.0 + extra[:, 8 + keys + k : 9 + keys + k]
            counts += jnp.where(ids == lanes, 1.0, 0.0)
        hot_grad += contract_rows(counts.astype(bf16), load_ref[at, din : din + width])
    if last:
        before.wait()
        out_ref[:, :part] = (tower_grad + before_ref[:, :part]).astype(bf16)
        out_ref[:, part:] = (hot_grad + before_ref[:, part:]).astype(bf16)
    else:
        out_ref[:, :part] = tower_grad
        out_ref[:, part:] = hot_grad


def columns(loads, half, head, keys, before=()):
    batch, wide = loads[0].shape
    rows, part = half.shape[1], head.shape[1]
    shape = (rows, half.shape[0])
    last = len(before) > 0
    return pl.pallas_call(
        functools.partial(columns_kernel, keys, last),
        out_shape=jax.ShapeDtypeStruct(shape, bf16 if last else f32),
        in_specs=[VM] + [HBM] * (1 + len(before) + len(loads)),
        out_specs=VM,
        scratch_shapes=[
            pltpu.VMEM((rows, part), bf16),
            pltpu.VMEM((batch * len(loads), wide), bf16),
            pltpu.SemaphoreType.DMA((2 + len(loads),)),
        ]
        + [pltpu.VMEM(shape, f32)] * len(before),
        compiler_params=ALONE,
        cost_estimate=cost(0.2),
        name="columns",
    )(head, half, *before, *loads)


def total_kernel(terms_ref, left_ref, right_ref):
    total = terms_ref[0].astype(f32)
    for n in range(1, terms_ref.shape[0]):
        total += terms_ref[n].astype(f32)
    half = left_ref.shape[1]
    left_ref[...] = total[:, :half]
    right_ref[...] = total[:, half:]


def total_of(terms):
    _, rows, wide = terms.shape
    return pl.pallas_call(
        total_kernel,
        out_shape=(jax.ShapeDtypeStruct((rows, wide // 2), f32),) * 2,
        in_specs=[VM],
        out_specs=(VM,) * 2,
        compiler_params=PARAMS,
        cost_estimate=cost(1),
        name="total",
    )(terms)


def lay_kernel(*refs):
    out0, out1 = refs[-2:]
    for axis, parts, out in (("z", refs[:4], out0), ("x", refs[4:8], out1)):
        step = parts[0].shape[0]
        for n, ref in enumerate(parts):
            at = lax.rem(lax.axis_index(axis) + n, 4) * step
            out[pl.ds(pl.multiple_of(at, step), step), :] = ref[...]


def lay(left, right):
    rows, wide = left[0].shape
    return pl.pallas_call(
        lay_kernel,
        out_shape=(jax.ShapeDtypeStruct((4 * rows, wide), f32),) * 2,
        in_specs=[VM] * 8,
        out_specs=(VM,) * 2,
        compiler_params=PARAMS,
        cost_estimate=cost(1),
        name="lay",
    )(*left, *right)


def update_kernel(l0, l1, l2, l3, r0, r1, r2, r3, *refs):
    w_ref, w_acc_ref, hot_ref, hot_acc_ref, nw_ref, nwa_ref, nh_ref, nha_ref, grad_ref = refs
    part = w_ref.shape[1]
    step, half = l0.shape
    piece = step // 4
    i = pl.program_id(0)
    for d, left in enumerate((l0, l1, l2, l3)):

        @pl.when(lax.rem(lax.axis_index("x") + d, 4) == i)
        def _():
            grad_ref[:, :half] = left[...]

    start = pl.multiple_of(i * piece, piece)
    for d, right in enumerate((r0, r1, r2, r3)):
        at = lax.rem(lax.axis_index("z") + d, 4) * piece
        grad_ref[pl.ds(pl.multiple_of(at, piece), piece), half:] = right[pl.ds(start, piece), :]
    nw, nwa = adagrad(w_ref[...], w_acc_ref[...], grad_ref[:, :part])
    nw_ref[...] = nw
    nwa_ref[...] = nwa
    nh, nha = adagrad(hot_ref[...], hot_acc_ref[...], grad_ref[:, part:])
    nh_ref[...] = nh
    nha_ref[...] = nha


def update(left, right, w, w_acc, hot, hot_acc):
    step, half = left[0].shape
    w_block = pl.BlockSpec((step, w.shape[1]), lambda i: (i, 0))
    hot_block = pl.BlockSpec((step, hot.shape[1]), lambda i: (i, 0))
    return pl.pallas_call(
        update_kernel,
        grid=(4,),
        in_specs=[VM] * 8
        + [w_block] * 2
        + [hot_block] * 2,
        out_specs=(w_block, w_block, hot_block, hot_block),
        out_shape=(jax.ShapeDtypeStruct(w.shape, f32),) * 2
        + (jax.ShapeDtypeStruct(hot.shape, f32),) * 2,
        scratch_shapes=[pltpu.VMEM((step, 2 * half), f32)],
        compiler_params=PARAMS,
        cost_estimate=cost(4),
        name="update",
    )(*left, *right, w, w_acc, hot, hot_acc)


def stage_kernel(*refs):
    count = len(refs) // 2
    sems = refs[-1]
    copies = [
        pltpu.make_async_copy(refs[n], refs[count + n], sems.at[n]) for n in range(count)
    ]
    for copy in copies:
        copy.start()
    for copy in copies:
        copy.wait()


def stage(values):
    return pl.pallas_call(
        stage_kernel,
        out_shape=tuple(jax.ShapeDtypeStruct(value.shape, value.dtype) for value in values),
        in_specs=[HBM] * len(values),
        out_specs=(VM,) * len(values),
        scratch_shapes=[pltpu.SemaphoreType.DMA((len(values),))],
        compiler_params=PARAMS,
        cost_estimate=cost(4),
        name="stage",
    )(*values)


def cold_kernel(asked_ref, grads_ref, table_ref, acc_ref, new_ref, new_acc_ref):
    step, width = table_ref.shape
    slots = grads_ref.shape[0]
    rows = iota((step, slots), 0) + pl.program_id(0) * step
    onehot = jnp.where(asked_ref[...] == rows, 1.0, 0.0).astype(bf16)
    grad = jnp.dot(onehot, grads_ref[...], preferred_element_type=f32)
    param, acc = adagrad(table_ref[...], acc_ref[...], grad)
    new_ref[...] = param
    new_acc_ref[...] = acc


def cold_update(asked, grads, table, acc):
    rows, width = table.shape
    slots = grads.shape[0]
    step = 256
    block = pl.BlockSpec((step, width), lambda i: (i, 0))
    return pl.pallas_call(
        cold_kernel,
        grid=(rows // step,),
        out_shape=(jax.ShapeDtypeStruct(table.shape, f32),) * 2,
        in_specs=[
            pl.BlockSpec((1, slots), lambda i: (0, 0)),
            pl.BlockSpec((slots, width), lambda i: (0, 0)),
            block,
            block,
        ],
        out_specs=(block, block),
        compiler_params=PARAMS,
        cost_estimate=cost(5),
        name="cold_update",
    )(asked, grads, table, acc)


def along(value, axis, by):
    return lax.ppermute(value, axis, [((i + by) % 4, i) for i in range(4)])


def around(value, axis):
    last, one = along(value, axis, 3), along(value, axis, 1)
    return value, one, along(value, axis, 2), last


def swap(value):
    return lax.ppermute(value, "core", [(0, 1), (1, 0)])


def on_device(
    hot_ids,
    cold_owner,
    cold_row,
    cold_exp,
    labels,
    head_w,
    hot_table,
    hot_acc,
    cold_table,
    cold_acc,
    tower_w,
    tower_acc,
):
    devices = math.prod(lax.axis_size(name) for name in ALL)
    y, core = lax.axis_index("y"), lax.axis_index("core")
    me = 2 * y + core
    batch, keys = hot_ids.shape
    hot_rows, width = hot_table.shape
    part = tower_w.shape[1]
    capacity = max(2, 2 * batch * cold_owner.shape[1] // devices)
    asks, place, scale, half, quarter = route(
        cold_owner.T, cold_row.T, cold_exp.T, hot_table, tower_w, devices, capacity
    )
    asked = lax.all_to_all(asks, ALL, split_axis=0, concat_axis=0, tiled=True)
    spread_mat = spread(place, scale, capacity)
    quarters = tuple(along(quarter, "y", by) for by in (1, 2, 3))
    counts = count_of(hot_ids, hot_rows)
    cold_half = cold_table.astype(bf16)
    asked, counts, cold_half, spread_mat = lax.optimization_barrier(
        (asked, counts, cold_half, spread_mat)
    )
    count = quarter.shape[0] // 2
    by_x = jnp.stack([value[:count] for value in quarters])
    by_z = jnp.stack([value[count:] for value in quarters])
    looked = lookup(asked, cold_half)
    xs = tuple(along(by_x, "x", by) for by in (1, 2, 3))
    zs = tuple(along(by_z, "z", by) for by in (1, 2, 3))
    returned = lax.all_to_all(
        looked.reshape(devices, capacity, width), ALL, split_axis=0, concat_axis=0, tiled=True
    ).reshape(-1, width)
    pieces = lax.optimization_barrier((half, by_x) + xs + (by_z,) + zs)
    pieces += tuple(swap(value) for value in pieces)
    hot_feat = hot_pooled(counts, pieces, width)
    heads = head_w.reshape(4, 2, part)
    turned = jnp.concatenate([heads, heads])
    turned = lax.dynamic_slice_in_dim(turned, y, 4, 0)
    head = jnp.concatenate(
        [lax.dynamic_slice_in_dim(turned, side, 1, 1).reshape(1, -1) for side in (core, 1 - core)],
        axis=1,
    )
    outgoing, load = tower(
        hot_feat, returned, spread_mat, head, labels[:, None], hot_ids, pieces
    )
    loads = around(load, "y")
    outgoing, loads = lax.optimization_barrier((outgoing, loads))
    incoming = lax.all_to_all(
        outgoing.reshape(devices, capacity, width), ALL, split_axis=0, concat_axis=0, tiled=True
    ).reshape(-1, width)
    loads += tuple(swap(part) for part in loads)
    head_part = lax.dynamic_slice(head_w, (me * part,), (part,))[None, :]
    own, one, two, last = loads[:4]
    early = columns((own, loads[4], one, last), half, head_part, keys)
    partial = columns((two,) + loads[5:], half, head_part, keys, (early,))
    partial, incoming = lax.optimization_barrier((partial, incoming))
    terms = lax.all_to_all(partial, ("x", "z"), split_axis=0, concat_axis=0, tiled=True)
    new_cold = cold_update(asked.reshape(1, -1), incoming, cold_table, cold_acc)
    terms, (new_cold, new_cold_acc) = lax.optimization_barrier((terms, new_cold))
    left, right = total_of(terms.reshape(16, -1, part + width))
    left, right = lay(around(left, "z"), around(right, "x"))
    params = (tower_w, tower_acc, hot_table, hot_acc)
    left, right, params = lax.optimization_barrier((left, right, params))
    params = stage(params)
    left, right = around(left, "x"), around(right, "z")
    new_w, new_w_acc, new_hot, new_hot_acc = update(
        left, right, *params
    )
    return (new_hot, new_hot_acc, new_cold, new_cold_acc, new_w, new_w_acc)


def solution(mesh):
    chips = mesh.devices.reshape(4, 2, 4, 4)
    mesh = jax.sharding.Mesh(chips, ALL)
    split = P(ALL, None)
    rows = P(TABLE, None)
    cols = P(None, TABLE)
    return jax.shard_map(
        on_device,
        mesh=mesh,
        in_specs=(split,) * 4 + (P(ALL), P(), rows, rows, split, split, cols, cols),
        out_specs=(rows, rows, split, split, cols, cols),
        check_vma=False,
    )
```

```python
import functools
import math

import jax
import jax.numpy as jnp
from jax import lax
from jax.experimental import pallas as pl
from jax.experimental.pallas import tpu as pltpu
from jax.sharding import PartitionSpec as P

learn_rate = 0.05
bf16 = jnp.bfloat16
f32 = jnp.float32
i32 = jnp.int32
ALL = ("y", "core", "z", "x")
TABLE = ("y", "core")
VM = pl.BlockSpec(memory_space=pltpu.VMEM)
HBM = pl.BlockSpec(memory_space=pltpu.HBM)
MIB = 1024 * 1024
PARAMS = pltpu.CompilerParams(vmem_limit_bytes=24 * MIB)
MOST = pltpu.CompilerParams(vmem_limit_bytes=57 * MIB)
ALONE = pltpu.CompilerParams(vmem_limit_bytes=60 * MIB)


def adagrad(param, accum, grad):
    new_accum = accum + grad * grad
    return (param - learn_rate * grad * lax.rsqrt(new_accum), new_accum)


def cost(us):
    return pl.CostEstimate(flops=int(us * 1e9), bytes_accessed=int(us * 3e6), transcendentals=0)


def iota(shape, axis):
    return lax.broadcasted_iota(i32, shape, axis)


def route_kernel(
    own_hbm,
    row_hbm,
    exp_hbm,
    hot_hbm,
    w_hbm,
    asks_ref,
    place_ref,
    scale_ref,
    half_ref,
    quarter_ref,
    own_ref,
    row_ref,
    exp_ref,
    hot_ref,
    w_ref,
    sems,
):
    pairs = (
        (own_hbm, own_ref),
        (row_hbm, row_ref),
        (exp_hbm, exp_ref),
        (hot_hbm, hot_ref),
        (w_hbm, w_ref),
    )
    copies = [pltpu.make_async_copy(a, b, sems.at[n]) for n, (a, b) in enumerate(pairs)]
    for copy in copies:
        copy.start()
    for copy in copies[:3]:
        copy.wait()
    keys, batch = own_ref.shape
    devices, capacity = asks_ref.shape
    owners = iota((devices, batch), 0)
    named = jnp.zeros((devices, batch), f32)
    rows = jnp.zeros((devices, batch), f32)
    scales = jnp.zeros((devices, batch), f32)
    expo = exp_ref[...]
    scale = jnp.where(expo == 0, 1.0, jnp.where(expo == 1, 0.5, 0.25))
    row = row_ref[...].astype(f32)
    own = own_ref[...]
    for k in range(keys):
        hit = own[k : k + 1, :] == owners
        named = jnp.where(hit, 1.0, named)
        rows = jnp.where(hit, row[k : k + 1, :], rows)
        scales = jnp.where(hit, scale[k : k + 1, :], scales)
    earlier = (iota((batch, batch), 0) < iota((batch, batch), 1)).astype(bf16)
    before = jnp.dot(named.astype(bf16), earlier, preferred_element_type=f32)
    place = jnp.where(named > 0, before + 1.0, 0.0)
    place_ref[...] = place
    scale_ref[...] = scales
    lanes = iota((devices, capacity), 1)
    asks = jnp.zeros((devices, capacity), f32)
    for s in range(capacity):
        col = jnp.sum(jnp.where(place == s + 1.0, rows, 0.0), axis=1, keepdims=True)
        asks = jnp.where(lanes == s, col, asks)
    asks_ref[...] = asks.astype(i32)
    din, rows_hot, width = w_ref.shape[0], hot_ref.shape[0] // 2, hot_ref.shape[1]
    copies[3].wait()
    half_ref[din:, :width] = hot_ref[:rows_hot, :].astype(bf16)
    half_ref[din:, width:] = hot_ref[rows_hot:, :].astype(bf16)
    copies[4].wait()
    half_ref[:din, :] = w_ref[...].astype(bf16)
    for which, axis in ((0, "x"), (1, "z")):
        at = lax.axis_index(axis)
        for first, count, to in ((0, din // 8, 0), (din, rows_hot // 8, din // 8)):
            start = pl.multiple_of(first + which * 4 * count + at * count, count)
            to += which * (din + rows_hot) // 8
            quarter_ref[to : to + count, :] = half_ref[pl.ds(start, count), :]


def route(own, row, expo, hot, w, devices, capacity):
    batch = own.shape[1]
    return pl.pallas_call(
        route_kernel,
        out_shape=(
            jax.ShapeDtypeStruct((devices, capacity), i32),
            jax.ShapeDtypeStruct((devices, batch), f32),
            jax.ShapeDtypeStruct((devices, batch), f32),
            jax.ShapeDtypeStruct((w.shape[0] + hot.shape[0] // 2, w.shape[1]), bf16),
            jax.ShapeDtypeStruct((w.shape[0] // 4 + hot.shape[0] // 8, w.shape[1]), bf16),
        ),
        in_specs=[HBM] * 5,
        out_specs=(VM,) * 5,
        scratch_shapes=[
            pltpu.VMEM(own.shape, i32),
            pltpu.VMEM(row.shape, i32),
            pltpu.VMEM(expo.shape, i32),
            pltpu.VMEM(hot.shape, f32),
            pltpu.VMEM(w.shape, f32),
            pltpu.SemaphoreType.DMA((5,)),
        ],
        compiler_params=ALONE,
        cost_estimate=cost(2),
        name="route",
    )(own, row, expo, hot, w)


def spread_kernel(place_ref, scale_ref, out_hbm, out_ref, sem):
    devices, batch = place_ref.shape
    capacity = out_ref.shape[0] // devices
    full = (devices, capacity, batch)
    slots = (iota(full, 1) + 1).astype(f32)
    place = jnp.broadcast_to(place_ref[...][:, None, :], full)
    scale = jnp.broadcast_to(scale_ref[...][:, None, :], full)
    out = jnp.where(place == slots, scale, 0.0)
    out_ref[...] = out.reshape(devices * capacity, batch).astype(bf16)
    copy = pltpu.make_async_copy(out_ref, out_hbm, sem)
    copy.start()
    copy.wait()


def spread(place, scale, capacity):
    devices, batch = place.shape
    shape = (devices * capacity, batch)
    return pl.pallas_call(
        spread_kernel,
        out_shape=jax.ShapeDtypeStruct(shape, bf16),
        in_specs=[VM] * 2,
        out_specs=HBM,
        scratch_shapes=[pltpu.VMEM(shape, bf16), pltpu.SemaphoreType.DMA],
        compiler_params=ALONE,
        cost_estimate=cost(1),
        name="spread",
    )(place, scale)


def lookup_kernel(asked_hbm, table_hbm, out_hbm, asked_ref, table_ref, out_ref, two, sems):
    devices, capacity = asked_ref.shape
    slots, width = out_ref.shape
    rows = table_ref.shape[0]
    first = pltpu.make_async_copy(asked_hbm, asked_ref, two.at[0])
    load = pltpu.make_async_copy(table_hbm, table_ref, two.at[1])
    first.start()
    load.start()
    first.wait()
    full = (devices, capacity, capacity)
    wide = jnp.broadcast_to(asked_ref[...].astype(f32)[:, None, :], full)
    kept = jnp.where(iota(full, 1) == iota(full, 2), wide, 0.0).reshape(slots, capacity)
    col = jnp.sum(kept, axis=1, keepdims=True).astype(i32)
    load.wait()
    step = 256
    copies = []
    for at in range(0, slots, step):
        hit = col[at : at + step] == iota((step, rows), 1)
        onehot = jnp.where(hit, 1.0, 0.0).astype(bf16)
        got = jnp.dot(onehot, table_ref[...], preferred_element_type=f32)
        out_ref[at : at + step, :] = got.astype(bf16)
        copies.append(
            pltpu.make_async_copy(
                out_ref.at[at : at + step], out_hbm.at[at : at + step], sems.at[at // step]
            )
        )
        copies[-1].start()
    for copy in copies:
        copy.wait()


def lookup(asked, table):
    devices, capacity = asked.shape
    shape = (devices * capacity, table.shape[1])
    return pl.pallas_call(
        lookup_kernel,
        out_shape=jax.ShapeDtypeStruct(shape, bf16),
        in_specs=[HBM, HBM],
        out_specs=HBM,
        scratch_shapes=[
            pltpu.VMEM(asked.shape, i32),
            pltpu.VMEM(table.shape, bf16),
            pltpu.VMEM(shape, bf16),
            pltpu.SemaphoreType.DMA((2,)),
            pltpu.SemaphoreType.DMA((shape[0] // 256,)),
        ],
        compiler_params=ALONE,
        cost_estimate=cost(3),
        name="lookup",
    )(asked, table)


def contract_rows(a, b):
    return lax.dot_general(a, b, (((0,), (0,)), ((), ())), preferred_element_type=f32)


def gather_copies(refs, first, buf, sems):
    x, z = lax.axis_index("x"), lax.axis_index("z")
    rows = buf.shape[2]
    count = rows // 8
    start = first // 8
    lists = []
    n = 0
    for side in range(2):
        half, *others = refs[9 * side : 9 * side + 9]
        copies = [
            pltpu.make_async_copy(half.at[first : first + rows], buf.at[side, 0], sems.at[n])
        ]
        n += 1
        for which, at in ((0, x), (1, z)):
            for d in range(4):
                to = lax.rem(at + d, 4) * count + which * 4 * count
                to_rows = pl.ds(pl.multiple_of(to, count), count)
                src = others[4 * which + d].at[:, start : start + count]
                dst = buf.at[side, 1:4, to_rows]
                copies.append(pltpu.make_async_copy(src, dst, sems.at[n]))
                n += 1
        lists.append(copies)
    for n, copies in enumerate(lists):
        copies[0].start(priority=n)
    for copies in lists:
        for n, copy in enumerate(copies[1:]):
            copy.start(priority=n % 2)
    return lists


COPIES = 2 * 9


def count_kernel(ids_ref, out_hbm, out_ref, sem):
    batch, keys = ids_ref.shape
    rows = out_ref.shape[1] // 8
    y, core = lax.axis_index("y"), lax.axis_index("core")
    ids = ids_ref[...]
    for t in range(8):
        side = core if t < 4 else 1 - core
        first = (2 * lax.rem(y + t, 4) + side) * rows
        lanes = iota((batch, rows), 1) + first
        counts = jnp.zeros((batch, rows), f32)
        for k in range(keys):
            counts += jnp.where(ids[:, k : k + 1] == lanes, 1.0, 0.0)
        out_ref[:, t * rows : (t + 1) * rows] = counts.astype(bf16)
    copy = pltpu.make_async_copy(out_ref, out_hbm, sem)
    copy.start()
    copy.wait()


def count_of(ids, rows):
    shape = (ids.shape[0], 8 * rows)
    return pl.pallas_call(
        count_kernel,
        out_shape=jax.ShapeDtypeStruct(shape, bf16),
        in_specs=[VM],
        out_specs=HBM,
        scratch_shapes=[pltpu.VMEM(shape, bf16), pltpu.SemaphoreType.DMA],
        compiler_params=ALONE,
        cost_estimate=cost(3),
        name="count",
    )(ids)


def hot_pool_kernel(counts_hbm, *refs):
    refs, (out_ref, buf, counts_ref, sem, sems) = refs[:-5], refs[-5:]
    _, _, rows, wide = buf.shape
    width = out_ref.shape[1]
    early = pltpu.make_async_copy(counts_hbm, counts_ref, sem)
    early.start()
    lists = gather_copies(refs, refs[0].shape[0] - rows, buf, sems)
    early.wait()
    pool = jnp.zeros(out_ref.shape, f32)
    for side, copies in enumerate(lists):
        for copy in copies:
            copy.wait()
        for y in range(4):
            at = (4 * side + y) * 2 * rows
            counts = counts_ref[:, at : at + 2 * rows]
            part = buf[side, y]
            pool += jnp.dot(counts[:, :rows], part[:, :width], preferred_element_type=f32)
            pool += jnp.dot(counts[:, rows:], part[:, width:], preferred_element_type=f32)
    out_ref[...] = pool.astype(bf16)


def hot_pooled(counts, pieces, width):
    wide = pieces[0].shape[1]
    rows = pieces[0].shape[0] - 2 * width
    return pl.pallas_call(
        hot_pool_kernel,
        out_shape=jax.ShapeDtypeStruct((counts.shape[0], width), bf16),
        in_specs=[HBM] * (1 + len(pieces)),
        out_specs=VM,
        scratch_shapes=[
            pltpu.VMEM((2, 4, rows, wide), bf16),
            pltpu.VMEM(counts.shape, bf16),
            pltpu.SemaphoreType.DMA,
            pltpu.SemaphoreType.DMA((COPIES,)),
        ],
        compiler_params=ALONE,
        cost_estimate=cost(0.1),
        name="hot_pool",
    )(counts, *pieces)


def tower_kernel(*refs):
    smalls, pieces, refs = refs[:6], refs[6:-14], refs[-14:]
    out_hbm, load_ref, pre_ref, sig_ref, *held, w_ref, out_ref, two, sems = refs
    small_copies = [
        pltpu.make_async_copy(a, b, two.at[n]) for n, (a, b) in enumerate(zip(smalls, held))
    ]
    for copy in small_copies:
        copy.start()
    hot_ref, returned_ref, spread_ref, head_ref, label_ref, ids_ref = held
    batch, width = hot_ref.shape
    _, _, din, part = w_ref.shape
    parts = 8
    keys = ids_ref.shape[1]
    lists = gather_copies(pieces, 0, w_ref, sems)
    for copy in small_copies:
        copy.wait()
    cold = contract_rows(spread_ref[...], returned_ref[...]).astype(bf16)
    feat = jnp.concatenate([hot_ref[...], cold], axis=1)
    logit = jnp.zeros((batch, 1), f32)
    waits = {0: lists[0][:1], 4: lists[1][:1], 1: lists[0][1:], 5: lists[1][1:]}
    for t in (0, 4, 1, 2, 3, 5, 6, 7):
        cols = slice(t * part, (t + 1) * part)
        for copy in waits.get(t, ()):
            copy.wait()
        pre = jnp.dot(feat, w_ref[t // 4, t % 4], preferred_element_type=f32)
        sig = jax.nn.sigmoid(pre)
        pre_ref[:, cols] = pre
        sig_ref[:, cols] = sig
        logit += jnp.sum(pre * sig * head_ref[:, cols], axis=1, keepdims=True)
    dlogit = jax.nn.sigmoid(logit) - label_ref[...]
    dfeat = jnp.zeros((batch, din), f32)
    for t in range(parts):
        cols = slice(t * part, (t + 1) * part)
        pre = pre_ref[:, cols]
        sig = sig_ref[:, cols]
        dpre = (dlogit * head_ref[:, cols] * sig * (1.0 + pre * (1.0 - sig))).astype(bf16)
        dfeat += lax.dot_general(
            dpre, w_ref[t // 4, t % 4], (((1,), (1,)), ((), ())), preferred_element_type=f32
        )
    dhot = dfeat[:, :width]
    dcold = dfeat[:, width:].astype(bf16)
    out_ref[...] = jnp.dot(spread_ref[...], dcold, preferred_element_type=f32).astype(bf16)
    last = pltpu.make_async_copy(out_ref, out_hbm, two.at[6])
    last.start()
    load_ref[:, :din] = feat
    load_ref[:, din : din + width] = dhot.astype(bf16)
    first = dlogit.astype(bf16).astype(f32)
    second = (dlogit - first).astype(bf16).astype(f32)
    third = dlogit - first - second
    lanes = iota((batch, 128), 1)
    extra = jnp.where(lanes == 0, first, 0.0)
    extra = jnp.where(lanes == 1, second, extra)
    extra = jnp.where(lanes == 2, third, extra)
    ids = ids_ref[...]
    high = lax.shift_right_logical(ids, 6)
    low = ids - high * 64
    high = high.astype(f32)
    low = low.astype(f32)
    for k in range(keys):
        extra = jnp.where(lanes == 8 + k, high[:, k : k + 1], extra)
        extra = jnp.where(lanes == 8 + keys + k, low[:, k : k + 1], extra)
    load_ref[:, din + width :] = extra.astype(bf16)
    last.wait()


def tower(hot, returned, spread_mat, head, label, ids, pieces):
    batch, width = hot.shape
    hidden = head.shape[1]
    smalls = (hot, returned, spread_mat, head, label, ids)
    return pl.pallas_call(
        tower_kernel,
        out_shape=(
            jax.ShapeDtypeStruct(returned.shape, bf16),
            jax.ShapeDtypeStruct((batch, 3 * width + 128), bf16),
        ),
        in_specs=[HBM] * (6 + len(pieces)),
        out_specs=(HBM, VM),
        scratch_shapes=[
            pltpu.VMEM((batch, hidden), f32),
            pltpu.VMEM((batch, hidden), f32),
        ]
        + [pltpu.VMEM(value.shape, value.dtype) for value in smalls]
        + [
            pltpu.VMEM((2, 4, 2 * width, hidden // 8), bf16),
            pltpu.VMEM(returned.shape, bf16),
            pltpu.SemaphoreType.DMA((7,)),
            pltpu.SemaphoreType.DMA((COPIES,)),
        ],
        compiler_params=MOST,
        cost_estimate=cost(6),
        name="tower",
    )(*smalls, *pieces)


def hold_kernel(in_ref, out_ref):
    pass


def hold(value):
    return pl.pallas_call(
        hold_kernel,
        out_shape=jax.ShapeDtypeStruct(value.shape, value.dtype),
        in_specs=[HBM],
        out_specs=HBM,
        input_output_aliases={0: 0},
        compiler_params=ALONE,
        cost_estimate=cost(30),
        name="hold",
    )(value)


def columns_kernel(keys, last, head_ref, half_hbm, *refs):
    if last:
        before_hbm, *refs = refs
        *loads, out_ref, half_ref, load_ref, sems, before_ref = refs
    else:
        *loads, out_ref, half_ref, load_ref, sems = refs
    din, part = half_ref.shape
    rows, width = din, din // 2
    batch = loads[0].shape[0]
    count = len(loads)
    first = pltpu.make_async_copy(half_hbm.at[:din], half_ref, sems.at[count])
    first.start()
    copies = [
        pltpu.make_async_copy(ref, load_ref.at[pl.ds(n * batch, batch)], sems.at[n])
        for n, ref in enumerate(loads)
    ]
    for copy in copies:
        copy.start()
    if last:
        before = pltpu.make_async_copy(before_hbm, before_ref, sems.at[count + 1])
        before.start()
    first.wait()
    base = (2 * lax.axis_index("y") + lax.axis_index("core")) * rows
    lanes = (iota((2 * batch, rows), 1) + base).astype(f32)
    tower_grad = jnp.zeros((din, part), f32)
    hot_grad = jnp.zeros((rows, width), f32)
    for n in range(0, count, 2):
        copies[n].wait()
        copies[n + 1].wait()
        at = slice(n * batch, (n + 2) * batch)
        feat = load_ref[at, :din]
        extra = load_ref[at, din + width :].astype(f32)
        dlogit = extra[:, 0:1] + extra[:, 1:2] + extra[:, 2:3]
        pre = jnp.dot(feat, half_ref[...], preferred_element_type=f32)
        sig = jax.nn.sigmoid(pre)
        dpre = (dlogit * head_ref[...] * sig * (1.0 + pre * (1.0 - sig))).astype(bf16)
        tower_grad += contract_rows(feat, dpre)
        counts = jnp.zeros((2 * batch, rows), f32)
        for k in range(keys):
            ids = extra[:, 8 + k : 9 + k] * 64.0 + extra[:, 8 + keys + k : 9 + keys + k]
            counts += jnp.where(ids == lanes, 1.0, 0.0)
        hot_grad += contract_rows(counts.astype(bf16), load_ref[at, din : din + width])
    if last:
        before.wait()
        out_ref[:, :part] = (tower_grad + before_ref[:, :part]).astype(bf16)
        out_ref[:, part:] = (hot_grad + before_ref[:, part:]).astype(bf16)
    else:
        out_ref[:, :part] = tower_grad
        out_ref[:, part:] = hot_grad


def columns(loads, half, head, keys, before=()):
    batch, wide = loads[0].shape
    rows, part = half.shape[1], head.shape[1]
    shape = (rows, half.shape[0])
    last = len(before) > 0
    return pl.pallas_call(
        functools.partial(columns_kernel, keys, last),
        out_shape=jax.ShapeDtypeStruct(shape, bf16 if last else f32),
        in_specs=[VM] + [HBM] * (1 + len(before) + len(loads)),
        out_specs=VM,
        scratch_shapes=[
            pltpu.VMEM((rows, part), bf16),
            pltpu.VMEM((batch * len(loads), wide), bf16),
            pltpu.SemaphoreType.DMA((2 + len(loads),)),
        ]
        + [pltpu.VMEM(shape, f32)] * len(before),
        compiler_params=ALONE,
        cost_estimate=cost(0.2),
        name="columns",
    )(head, half, *before, *loads)


def total_kernel(terms_ref, left_ref, right_ref):
    total = terms_ref[0].astype(f32)
    for n in range(1, terms_ref.shape[0]):
        total += terms_ref[n].astype(f32)
    half = left_ref.shape[1]
    left_ref[...] = total[:, :half]
    right_ref[...] = total[:, half:]


def total_of(terms):
    _, rows, wide = terms.shape
    return pl.pallas_call(
        total_kernel,
        out_shape=(jax.ShapeDtypeStruct((rows, wide // 2), f32),) * 2,
        in_specs=[VM],
        out_specs=(VM,) * 2,
        compiler_params=PARAMS,
        cost_estimate=cost(1),
        name="total",
    )(terms)


def lay_kernel(*refs):
    out0, out1 = refs[-2:]
    for axis, parts, out in (("z", refs[:4], out0), ("x", refs[4:8], out1)):
        step = parts[0].shape[0]
        for n, ref in enumerate(parts):
            at = lax.rem(lax.axis_index(axis) + n, 4) * step
            out[pl.ds(pl.multiple_of(at, step), step), :] = ref[...]


def lay(left, right):
    rows, wide = left[0].shape
    return pl.pallas_call(
        lay_kernel,
        out_shape=(jax.ShapeDtypeStruct((4 * rows, wide), f32),) * 2,
        in_specs=[VM] * 8,
        out_specs=(VM,) * 2,
        compiler_params=PARAMS,
        cost_estimate=cost(1),
        name="lay",
    )(*left, *right)


def update_kernel(l0, l1, l2, l3, r0, r1, r2, r3, *refs):
    w_ref, w_acc_ref, hot_ref, hot_acc_ref, nw_ref, nwa_ref, nh_ref, nha_ref, grad_ref = refs
    part = w_ref.shape[1]
    step, half = l0.shape
    piece = step // 4
    i = pl.program_id(0)
    for d, left in enumerate((l0, l1, l2, l3)):

        @pl.when(lax.rem(lax.axis_index("x") + d, 4) == i)
        def _():
            grad_ref[:, :half] = left[...]

    start = pl.multiple_of(i * piece, piece)
    for d, right in enumerate((r0, r1, r2, r3)):
        at = lax.rem(lax.axis_index("z") + d, 4) * piece
        grad_ref[pl.ds(pl.multiple_of(at, piece), piece), half:] = right[pl.ds(start, piece), :]
    nw, nwa = adagrad(w_ref[...], w_acc_ref[...], grad_ref[:, :part])
    nw_ref[...] = nw
    nwa_ref[...] = nwa
    nh, nha = adagrad(hot_ref[...], hot_acc_ref[...], grad_ref[:, part:])
    nh_ref[...] = nh
    nha_ref[...] = nha


def update(left, right, w, w_acc, hot, hot_acc):
    step, half = left[0].shape
    w_block = pl.BlockSpec((step, w.shape[1]), lambda i: (i, 0))
    hot_block = pl.BlockSpec((step, hot.shape[1]), lambda i: (i, 0))
    return pl.pallas_call(
        update_kernel,
        grid=(4,),
        in_specs=[VM] * 8
        + [w_block] * 2
        + [hot_block] * 2,
        out_specs=(w_block, w_block, hot_block, hot_block),
        out_shape=(jax.ShapeDtypeStruct(w.shape, f32),) * 2
        + (jax.ShapeDtypeStruct(hot.shape, f32),) * 2,
        scratch_shapes=[pltpu.VMEM((step, 2 * half), f32)],
        compiler_params=PARAMS,
        cost_estimate=cost(4),
        name="update",
    )(*left, *right, w, w_acc, hot, hot_acc)


def stage_kernel(*refs):
    count = len(refs) // 2
    sems = refs[-1]
    copies = [
        pltpu.make_async_copy(refs[n], refs[count + n], sems.at[n]) for n in range(count)
    ]
    for copy in copies:
        copy.start()
    for copy in copies:
        copy.wait()


def stage(values):
    return pl.pallas_call(
        stage_kernel,
        out_shape=tuple(jax.ShapeDtypeStruct(value.shape, value.dtype) for value in values),
        in_specs=[HBM] * len(values),
        out_specs=(VM,) * len(values),
        scratch_shapes=[pltpu.SemaphoreType.DMA((len(values),))],
        compiler_params=PARAMS,
        cost_estimate=cost(4),
        name="stage",
    )(*values)


def cold_kernel(asked_ref, grads_ref, table_ref, acc_ref, new_ref, new_acc_ref):
    step, width = table_ref.shape
    slots = grads_ref.shape[0]
    rows = iota((step, slots), 0) + pl.program_id(0) * step
    onehot = jnp.where(asked_ref[...] == rows, 1.0, 0.0).astype(bf16)
    grad = jnp.dot(onehot, grads_ref[...], preferred_element_type=f32)
    param, acc = adagrad(table_ref[...], acc_ref[...], grad)
    new_ref[...] = param
    new_acc_ref[...] = acc


def cold_update(asked, grads, table, acc):
    rows, width = table.shape
    slots = grads.shape[0]
    step = 256
    block = pl.BlockSpec((step, width), lambda i: (i, 0))
    return pl.pallas_call(
        cold_kernel,
        grid=(rows // step,),
        out_shape=(jax.ShapeDtypeStruct(table.shape, f32),) * 2,
        in_specs=[
            pl.BlockSpec((1, slots), lambda i: (0, 0)),
            pl.BlockSpec((slots, width), lambda i: (0, 0)),
            block,
            block,
        ],
        out_specs=(block, block),
        compiler_params=PARAMS,
        cost_estimate=cost(5),
        name="cold_update",
    )(asked, grads, table, acc)


def along(value, axis, by):
    return lax.ppermute(value, axis, [((i + by) % 4, i) for i in range(4)])


def around(value, axis):
    last, one = along(value, axis, 3), along(value, axis, 1)
    return value, one, along(value, axis, 2), last


def swap(value):
    return lax.ppermute(value, "core", [(0, 1), (1, 0)])


def on_device(
    hot_ids,
    cold_owner,
    cold_row,
    cold_exp,
    labels,
    head_w,
    hot_table,
    hot_acc,
    cold_table,
    cold_acc,
    tower_w,
    tower_acc,
):
    devices = math.prod(lax.axis_size(name) for name in ALL)
    y, core = lax.axis_index("y"), lax.axis_index("core")
    me = 2 * y + core
    batch, keys = hot_ids.shape
    hot_rows, width = hot_table.shape
    part = tower_w.shape[1]
    capacity = max(2, 2 * batch * cold_owner.shape[1] // devices)
    asks, place, scale, half, quarter = route(
        cold_owner.T, cold_row.T, cold_exp.T, hot_table, tower_w, devices, capacity
    )
    asked = lax.all_to_all(asks, ALL, split_axis=0, concat_axis=0, tiled=True)
    spread_mat = spread(place, scale, capacity)
    quarters = tuple(along(quarter, "y", by) for by in (1, 2, 3))
    counts = count_of(hot_ids, hot_rows)
    cold_half = cold_table.astype(bf16)
    asked, counts, cold_half = lax.optimization_barrier((asked, counts, cold_half))
    count = quarter.shape[0] // 2
    by_x = jnp.stack([value[:count] for value in quarters])
    by_z = jnp.stack([value[count:] for value in quarters])
    looked = lookup(asked, cold_half)
    xs = tuple(along(by_x, "x", by) for by in (1, 2, 3))
    zs = tuple(along(by_z, "z", by) for by in (1, 2, 3))
    returned = lax.all_to_all(
        looked.reshape(devices, capacity, width), ALL, split_axis=0, concat_axis=0, tiled=True
    ).reshape(-1, width)
    pieces = lax.optimization_barrier((half, by_x) + xs + (by_z,) + zs)
    pieces += tuple(swap(value) for value in pieces)
    hot_feat = hot_pooled(counts, pieces, width)
    heads = head_w.reshape(4, 2, part)
    turned = jnp.concatenate([heads, heads])
    turned = lax.dynamic_slice_in_dim(turned, y, 4, 0)
    head = jnp.concatenate(
        [lax.dynamic_slice_in_dim(turned, side, 1, 1).reshape(1, -1) for side in (core, 1 - core)],
        axis=1,
    )
    outgoing, load = tower(
        hot_feat, returned, spread_mat, head, labels[:, None], hot_ids, pieces
    )
    loads = around(load, "y")
    outgoing, loads = lax.optimization_barrier((outgoing, loads))
    incoming = lax.all_to_all(
        outgoing.reshape(devices, capacity, width), ALL, split_axis=0, concat_axis=0, tiled=True
    ).reshape(-1, width)
    loads += tuple(swap(part) for part in loads)
    head_part = lax.dynamic_slice(head_w, (me * part,), (part,))[None, :]
    own, one, two, last = loads[:4]
    early = columns((own, loads[4], one, last), half, head_part, keys)
    partial = columns((two,) + loads[5:], half, head_part, keys, (early,))
    partial, incoming = lax.optimization_barrier((partial, incoming))
    terms = lax.all_to_all(partial, ("x", "z"), split_axis=0, concat_axis=0, tiled=True)
    new_cold = cold_update(asked.reshape(1, -1), incoming, cold_table, cold_acc)
    terms, (new_cold, new_cold_acc) = lax.optimization_barrier((terms, new_cold))
    left, right = total_of(terms.reshape(16, -1, part + width))
    left, right = lay(around(left, "z"), around(right, "x"))
    params = (tower_w, tower_acc, hot_table, hot_acc)
    left, right, params = lax.optimization_barrier((left, right, params))
    params = stage(params)
    left, right = around(left, "x"), around(right, "z")
    new_w, new_w_acc, new_hot, new_hot_acc = update(
        left, right, *params
    )
    return (new_hot, new_hot_acc, new_cold, new_cold_acc, new_w, new_w_acc)


def solution(mesh):
    chips = mesh.devices.reshape(4, 2, 4, 4)
    mesh = jax.sharding.Mesh(chips, ALL)
    split = P(ALL, None)
    rows = P(TABLE, None)
    cols = P(None, TABLE)
    return jax.shard_map(
        on_device,
        mesh=mesh,
        in_specs=(split,) * 4 + (P(ALL), P(), rows, rows, split, split, cols, cols),
        out_specs=(rows, rows, split, split, cols, cols),
        check_vma=False,
    )
```

```python
import functools
import math

import jax
import jax.numpy as jnp
from jax import lax
from jax.experimental import pallas as pl
from jax.experimental.pallas import tpu as pltpu
from jax.sharding import PartitionSpec as P

learn_rate = 0.05
bf16 = jnp.bfloat16
f32 = jnp.float32
i32 = jnp.int32
ALL = ("y", "core", "z", "x")
TABLE = ("y", "core")
VM = pl.BlockSpec(memory_space=pltpu.VMEM)
HBM = pl.BlockSpec(memory_space=pltpu.HBM)
MIB = 1024 * 1024
PARAMS = pltpu.CompilerParams(vmem_limit_bytes=24 * MIB)
MOST = pltpu.CompilerParams(vmem_limit_bytes=57 * MIB)
ALONE = pltpu.CompilerParams(vmem_limit_bytes=60 * MIB)


def adagrad(param, accum, grad):
    new_accum = accum + grad * grad
    return (param - learn_rate * grad * lax.rsqrt(new_accum), new_accum)


def cost(us):
    return pl.CostEstimate(flops=int(us * 1e9), bytes_accessed=int(us * 3e6), transcendentals=0)


def iota(shape, axis):
    return lax.broadcasted_iota(i32, shape, axis)


def route_kernel(
    own_hbm,
    row_hbm,
    exp_hbm,
    hot_hbm,
    w_hbm,
    asks_ref,
    place_ref,
    scale_ref,
    half_ref,
    quarter_ref,
    own_ref,
    row_ref,
    exp_ref,
    hot_ref,
    w_ref,
    sems,
):
    pairs = (
        (own_hbm, own_ref),
        (row_hbm, row_ref),
        (exp_hbm, exp_ref),
        (hot_hbm, hot_ref),
        (w_hbm, w_ref),
    )
    copies = [pltpu.make_async_copy(a, b, sems.at[n]) for n, (a, b) in enumerate(pairs)]
    for copy in copies:
        copy.start()
    for copy in copies[:3]:
        copy.wait()
    keys, batch = own_ref.shape
    devices, capacity = asks_ref.shape
    owners = iota((devices, batch), 0)
    named = jnp.zeros((devices, batch), f32)
    rows = jnp.zeros((devices, batch), f32)
    scales = jnp.zeros((devices, batch), f32)
    expo = exp_ref[...]
    scale = jnp.where(expo == 0, 1.0, jnp.where(expo == 1, 0.5, 0.25))
    row = row_ref[...].astype(f32)
    own = own_ref[...]
    for k in range(keys):
        hit = own[k : k + 1, :] == owners
        named = jnp.where(hit, 1.0, named)
        rows = jnp.where(hit, row[k : k + 1, :], rows)
        scales = jnp.where(hit, scale[k : k + 1, :], scales)
    earlier = (iota((batch, batch), 0) < iota((batch, batch), 1)).astype(bf16)
    before = jnp.dot(named.astype(bf16), earlier, preferred_element_type=f32)
    place = jnp.where(named > 0, before + 1.0, 0.0)
    place_ref[...] = place
    scale_ref[...] = scales
    lanes = iota((devices, capacity), 1)
    asks = jnp.zeros((devices, capacity), f32)
    for s in range(capacity):
        col = jnp.sum(jnp.where(place == s + 1.0, rows, 0.0), axis=1, keepdims=True)
        asks = jnp.where(lanes == s, col, asks)
    asks_ref[...] = asks.astype(i32)
    din, rows_hot, width = w_ref.shape[0], hot_ref.shape[0] // 2, hot_ref.shape[1]
    copies[3].wait()
    half_ref[din:, :width] = hot_ref[:rows_hot, :].astype(bf16)
    half_ref[din:, width:] = hot_ref[rows_hot:, :].astype(bf16)
    copies[4].wait()
    half_ref[:din, :] = w_ref[...].astype(bf16)
    for which, axis in ((0, "x"), (1, "z")):
        at = lax.axis_index(axis)
        for first, count, to in ((0, din // 8, 0), (din, rows_hot // 8, din // 8)):
            start = pl.multiple_of(first + which * 4 * count + at * count, count)
            to += which * (din + rows_hot) // 8
            quarter_ref[to : to + count, :] = half_ref[pl.ds(start, count), :]


def route(own, row, expo, hot, w, devices, capacity):
    batch = own.shape[1]
    return pl.pallas_call(
        route_kernel,
        out_shape=(
            jax.ShapeDtypeStruct((devices, capacity), i32),
            jax.ShapeDtypeStruct((devices, batch), f32),
            jax.ShapeDtypeStruct((devices, batch), f32),
            jax.ShapeDtypeStruct((w.shape[0] + hot.shape[0] // 2, w.shape[1]), bf16),
            jax.ShapeDtypeStruct((w.shape[0] // 4 + hot.shape[0] // 8, w.shape[1]), bf16),
        ),
        in_specs=[HBM] * 5,
        out_specs=(VM,) * 5,
        scratch_shapes=[
            pltpu.VMEM(own.shape, i32),
            pltpu.VMEM(row.shape, i32),
            pltpu.VMEM(expo.shape, i32),
            pltpu.VMEM(hot.shape, f32),
            pltpu.VMEM(w.shape, f32),
            pltpu.SemaphoreType.DMA((5,)),
        ],
        compiler_params=ALONE,
        cost_estimate=cost(2),
        name="route",
    )(own, row, expo, hot, w)


def spread_kernel(place_ref, scale_ref, out_hbm, out_ref, sem):
    devices, batch = place_ref.shape
    capacity = out_ref.shape[0] // devices
    full = (devices, capacity, batch)
    slots = (iota(full, 1) + 1).astype(f32)
    place = jnp.broadcast_to(place_ref[...][:, None, :], full)
    scale = jnp.broadcast_to(scale_ref[...][:, None, :], full)
    out = jnp.where(place == slots, scale, 0.0)
    out_ref[...] = out.reshape(devices * capacity, batch).astype(bf16)
    copy = pltpu.make_async_copy(out_ref, out_hbm, sem)
    copy.start()
    copy.wait()


def spread(place, scale, capacity):
    devices, batch = place.shape
    shape = (devices * capacity, batch)
    return pl.pallas_call(
        spread_kernel,
        out_shape=jax.ShapeDtypeStruct(shape, bf16),
        in_specs=[VM] * 2,
        out_specs=HBM,
        scratch_shapes=[pltpu.VMEM(shape, bf16), pltpu.SemaphoreType.DMA],
        compiler_params=ALONE,
        cost_estimate=cost(1),
        name="spread",
    )(place, scale)


def lookup_kernel(asked_hbm, table_hbm, out_hbm, asked_ref, table_ref, out_ref, two, sems):
    devices, capacity = asked_ref.shape
    slots, width = out_ref.shape
    rows = table_ref.shape[0]
    first = pltpu.make_async_copy(asked_hbm, asked_ref, two.at[0])
    load = pltpu.make_async_copy(table_hbm, table_ref, two.at[1])
    first.start()
    load.start()
    first.wait()
    full = (devices, capacity, capacity)
    wide = jnp.broadcast_to(asked_ref[...].astype(f32)[:, None, :], full)
    kept = jnp.where(iota(full, 1) == iota(full, 2), wide, 0.0).reshape(slots, capacity)
    col = jnp.sum(kept, axis=1, keepdims=True).astype(i32)
    load.wait()
    step = 256
    copies = []
    for at in range(0, slots, step):
        hit = col[at : at + step] == iota((step, rows), 1)
        onehot = jnp.where(hit, 1.0, 0.0).astype(bf16)
        got = jnp.dot(onehot, table_ref[...], preferred_element_type=f32)
        out_ref[at : at + step, :] = got.astype(bf16)
        copies.append(
            pltpu.make_async_copy(
                out_ref.at[at : at + step], out_hbm.at[at : at + step], sems.at[at // step]
            )
        )
        copies[-1].start()
    for copy in copies:
        copy.wait()


def lookup(asked, table):
    devices, capacity = asked.shape
    shape = (devices * capacity, table.shape[1])
    return pl.pallas_call(
        lookup_kernel,
        out_shape=jax.ShapeDtypeStruct(shape, bf16),
        in_specs=[HBM, HBM],
        out_specs=HBM,
        scratch_shapes=[
            pltpu.VMEM(asked.shape, i32),
            pltpu.VMEM(table.shape, bf16),
            pltpu.VMEM(shape, bf16),
            pltpu.SemaphoreType.DMA((2,)),
            pltpu.SemaphoreType.DMA((shape[0] // 256,)),
        ],
        compiler_params=ALONE,
        cost_estimate=cost(3),
        name="lookup",
    )(asked, table)


def contract_rows(a, b):
    return lax.dot_general(a, b, (((0,), (0,)), ((), ())), preferred_element_type=f32)


def gather_copies(refs, first, buf, sems):
    x, z = lax.axis_index("x"), lax.axis_index("z")
    rows = buf.shape[2]
    count = rows // 8
    start = first // 8
    lists = []
    n = 0
    for side in range(2):
        half, *others = refs[9 * side : 9 * side + 9]
        copies = [
            pltpu.make_async_copy(half.at[first : first + rows], buf.at[side, 0], sems.at[n])
        ]
        n += 1
        for which, at in ((0, x), (1, z)):
            for d in range(4):
                to = lax.rem(at + d, 4) * count + which * 4 * count
                to_rows = pl.ds(pl.multiple_of(to, count), count)
                src = others[4 * which + d].at[:, start : start + count]
                dst = buf.at[side, 1:4, to_rows]
                copies.append(pltpu.make_async_copy(src, dst, sems.at[n]))
                n += 1
        lists.append(copies)
    for n, copies in enumerate(lists):
        copies[0].start(priority=n)
    for copies in lists:
        for n, copy in enumerate(copies[1:]):
            copy.start(priority=n % 2)
    return lists


COPIES = 2 * 9


def count_kernel(ids_ref, out_hbm, out_ref, sem):
    batch, keys = ids_ref.shape
    rows = out_ref.shape[1] // 8
    y, core = lax.axis_index("y"), lax.axis_index("core")
    ids = ids_ref[...]
    for t in range(8):
        side = core if t < 4 else 1 - core
        first = (2 * lax.rem(y + t, 4) + side) * rows
        lanes = iota((batch, rows), 1) + first
        counts = jnp.zeros((batch, rows), f32)
        for k in range(keys):
            counts += jnp.where(ids[:, k : k + 1] == lanes, 1.0, 0.0)
        out_ref[:, t * rows : (t + 1) * rows] = counts.astype(bf16)
    copy = pltpu.make_async_copy(out_ref, out_hbm, sem)
    copy.start()
    copy.wait()


def count_of(ids, rows):
    shape = (ids.shape[0], 8 * rows)
    return pl.pallas_call(
        count_kernel,
        out_shape=jax.ShapeDtypeStruct(shape, bf16),
        in_specs=[VM],
        out_specs=HBM,
        scratch_shapes=[pltpu.VMEM(shape, bf16), pltpu.SemaphoreType.DMA],
        compiler_params=ALONE,
        cost_estimate=cost(3),
        name="count",
    )(ids)


def hot_pool_kernel(counts_hbm, *refs):
    refs, (out_ref, buf, counts_ref, sem, sems) = refs[:-5], refs[-5:]
    _, _, rows, wide = buf.shape
    width = out_ref.shape[1]
    early = pltpu.make_async_copy(counts_hbm, counts_ref, sem)
    early.start()
    lists = gather_copies(refs, refs[0].shape[0] - rows, buf, sems)
    early.wait()
    pool = jnp.zeros(out_ref.shape, f32)
    for side, copies in enumerate(lists):
        for copy in copies:
            copy.wait()
        for y in range(4):
            at = (4 * side + y) * 2 * rows
            counts = counts_ref[:, at : at + 2 * rows]
            part = buf[side, y]
            pool += jnp.dot(counts[:, :rows], part[:, :width], preferred_element_type=f32)
            pool += jnp.dot(counts[:, rows:], part[:, width:], preferred_element_type=f32)
    out_ref[...] = pool.astype(bf16)


def hot_pooled(counts, pieces, width):
    wide = pieces[0].shape[1]
    rows = pieces[0].shape[0] - 2 * width
    return pl.pallas_call(
        hot_pool_kernel,
        out_shape=jax.ShapeDtypeStruct((counts.shape[0], width), bf16),
        in_specs=[HBM] * (1 + len(pieces)),
        out_specs=VM,
        scratch_shapes=[
            pltpu.VMEM((2, 4, rows, wide), bf16),
            pltpu.VMEM(counts.shape, bf16),
            pltpu.SemaphoreType.DMA,
            pltpu.SemaphoreType.DMA((COPIES,)),
        ],
        compiler_params=ALONE,
        cost_estimate=cost(0.1),
        name="hot_pool",
    )(counts, *pieces)


def tower_kernel(*refs):
    smalls, pieces, refs = refs[:6], refs[6:-14], refs[-14:]
    out_hbm, load_ref, pre_ref, sig_ref, *held, w_ref, out_ref, two, sems = refs
    small_copies = [
        pltpu.make_async_copy(a, b, two.at[n]) for n, (a, b) in enumerate(zip(smalls, held))
    ]
    for copy in small_copies:
        copy.start()
    hot_ref, returned_ref, spread_ref, head_ref, label_ref, ids_ref = held
    batch, width = hot_ref.shape
    _, _, din, part = w_ref.shape
    parts = 8
    keys = ids_ref.shape[1]
    lists = gather_copies(pieces, 0, w_ref, sems)
    for copy in small_copies:
        copy.wait()
    cold = contract_rows(spread_ref[...], returned_ref[...]).astype(bf16)
    feat = jnp.concatenate([hot_ref[...], cold], axis=1)
    logit = jnp.zeros((batch, 1), f32)
    waits = {0: lists[0][:1], 4: lists[1][:1], 1: lists[0][1:], 5: lists[1][1:]}
    for t in (0, 4, 1, 2, 3, 5, 6, 7):
        cols = slice(t * part, (t + 1) * part)
        for copy in waits.get(t, ()):
            copy.wait()
        pre = jnp.dot(feat, w_ref[t // 4, t % 4], preferred_element_type=f32)
        sig = jax.nn.sigmoid(pre)
        pre_ref[:, cols] = pre
        sig_ref[:, cols] = sig
        logit += jnp.sum(pre * sig * head_ref[:, cols], axis=1, keepdims=True)
    dlogit = jax.nn.sigmoid(logit) - label_ref[...]
    dfeat = jnp.zeros((batch, din), f32)
    for t in range(parts):
        cols = slice(t * part, (t + 1) * part)
        pre = pre_ref[:, cols]
        sig = sig_ref[:, cols]
        dpre = (dlogit * head_ref[:, cols] * sig * (1.0 + pre * (1.0 - sig))).astype(bf16)
        dfeat += lax.dot_general(
            dpre, w_ref[t // 4, t % 4], (((1,), (1,)), ((), ())), preferred_element_type=f32
        )
    dhot = dfeat[:, :width]
    dcold = dfeat[:, width:].astype(bf16)
    stores = []
    step = out_ref.shape[0] // 4
    for n in range(4):
        at = slice(n * step, (n + 1) * step)
        out = jnp.dot(spread_ref[at, :], dcold, preferred_element_type=f32)
        out_ref[at, :] = out.astype(bf16)
        stores.append(pltpu.make_async_copy(out_ref.at[at], out_hbm.at[at], two.at[6 + n]))
        stores[n].start(priority=n % 2)
    load_ref[:, :din] = feat
    load_ref[:, din : din + width] = dhot.astype(bf16)
    first = dlogit.astype(bf16).astype(f32)
    second = (dlogit - first).astype(bf16).astype(f32)
    third = dlogit - first - second
    lanes = iota((batch, 128), 1)
    extra = jnp.where(lanes == 0, first, 0.0)
    extra = jnp.where(lanes == 1, second, extra)
    extra = jnp.where(lanes == 2, third, extra)
    ids = ids_ref[...]
    high = lax.shift_right_logical(ids, 6)
    low = ids - high * 64
    high = high.astype(f32)
    low = low.astype(f32)
    for k in range(keys):
        extra = jnp.where(lanes == 8 + k, high[:, k : k + 1], extra)
        extra = jnp.where(lanes == 8 + keys + k, low[:, k : k + 1], extra)
    load_ref[:, din + width :] = extra.astype(bf16)
    for store in stores:
        store.wait()


def tower(hot, returned, spread_mat, head, label, ids, pieces):
    batch, width = hot.shape
    hidden = head.shape[1]
    smalls = (hot, returned, spread_mat, head, label, ids)
    return pl.pallas_call(
        tower_kernel,
        out_shape=(
            jax.ShapeDtypeStruct(returned.shape, bf16),
            jax.ShapeDtypeStruct((batch, 3 * width + 128), bf16),
        ),
        in_specs=[HBM] * (6 + len(pieces)),
        out_specs=(HBM, VM),
        scratch_shapes=[
            pltpu.VMEM((batch, hidden), f32),
            pltpu.VMEM((batch, hidden), f32),
        ]
        + [pltpu.VMEM(value.shape, value.dtype) for value in smalls]
        + [
            pltpu.VMEM((2, 4, 2 * width, hidden // 8), bf16),
            pltpu.VMEM(returned.shape, bf16),
            pltpu.SemaphoreType.DMA((10,)),
            pltpu.SemaphoreType.DMA((COPIES,)),
        ],
        compiler_params=MOST,
        cost_estimate=cost(6),
        name="tower",
    )(*smalls, *pieces)


def hold_kernel(in_ref, out_ref):
    pass


def hold(value):
    return pl.pallas_call(
        hold_kernel,
        out_shape=jax.ShapeDtypeStruct(value.shape, value.dtype),
        in_specs=[HBM],
        out_specs=HBM,
        input_output_aliases={0: 0},
        compiler_params=ALONE,
        cost_estimate=cost(30),
        name="hold",
    )(value)


def columns_kernel(keys, last, head_ref, half_hbm, *refs):
    if last:
        before_hbm, *refs = refs
        *loads, out_ref, half_ref, load_ref, sems, before_ref = refs
    else:
        *loads, out_ref, half_ref, load_ref, sems = refs
    din, part = half_ref.shape
    rows, width = din, din // 2
    batch = loads[0].shape[0]
    count = len(loads)
    first = pltpu.make_async_copy(half_hbm.at[:din], half_ref, sems.at[count])
    first.start()
    copies = [
        pltpu.make_async_copy(ref, load_ref.at[pl.ds(n * batch, batch)], sems.at[n])
        for n, ref in enumerate(loads)
    ]
    for copy in copies:
        copy.start()
    if last:
        before = pltpu.make_async_copy(before_hbm, before_ref, sems.at[count + 1])
        before.start()
    first.wait()
    base = (2 * lax.axis_index("y") + lax.axis_index("core")) * rows
    lanes = (iota((2 * batch, rows), 1) + base).astype(f32)
    tower_grad = jnp.zeros((din, part), f32)
    hot_grad = jnp.zeros((rows, width), f32)
    for n in range(0, count, 2):
        copies[n].wait()
        copies[n + 1].wait()
        at = slice(n * batch, (n + 2) * batch)
        feat = load_ref[at, :din]
        extra = load_ref[at, din + width :].astype(f32)
        dlogit = extra[:, 0:1] + extra[:, 1:2] + extra[:, 2:3]
        pre = jnp.dot(feat, half_ref[...], preferred_element_type=f32)
        sig = jax.nn.sigmoid(pre)
        dpre = (dlogit * head_ref[...] * sig * (1.0 + pre * (1.0 - sig))).astype(bf16)
        tower_grad += contract_rows(feat, dpre)
        counts = jnp.zeros((2 * batch, rows), f32)
        for k in range(keys):
            ids = extra[:, 8 + k : 9 + k] * 64.0 + extra[:, 8 + keys + k : 9 + keys + k]
            counts += jnp.where(ids == lanes, 1.0, 0.0)
        hot_grad += contract_rows(counts.astype(bf16), load_ref[at, din : din + width])
    if last:
        before.wait()
        out_ref[:, :part] = (tower_grad + before_ref[:, :part]).astype(bf16)
        out_ref[:, part:] = (hot_grad + before_ref[:, part:]).astype(bf16)
    else:
        out_ref[:, :part] = tower_grad
        out_ref[:, part:] = hot_grad


def columns(loads, half, head, keys, before=()):
    batch, wide = loads[0].shape
    rows, part = half.shape[1], head.shape[1]
    shape = (rows, half.shape[0])
    last = len(before) > 0
    return pl.pallas_call(
        functools.partial(columns_kernel, keys, last),
        out_shape=jax.ShapeDtypeStruct(shape, bf16 if last else f32),
        in_specs=[VM] + [HBM] * (1 + len(before) + len(loads)),
        out_specs=VM,
        scratch_shapes=[
            pltpu.VMEM((rows, part), bf16),
            pltpu.VMEM((batch * len(loads), wide), bf16),
            pltpu.SemaphoreType.DMA((2 + len(loads),)),
        ]
        + [pltpu.VMEM(shape, f32)] * len(before),
        compiler_params=ALONE,
        cost_estimate=cost(0.2),
        name="columns",
    )(head, half, *before, *loads)


def total_kernel(terms_ref, left_ref, right_ref):
    total = terms_ref[0].astype(f32)
    for n in range(1, terms_ref.shape[0]):
        total += terms_ref[n].astype(f32)
    half = left_ref.shape[1]
    left_ref[...] = total[:, :half]
    right_ref[...] = total[:, half:]


def total_of(terms):
    _, rows, wide = terms.shape
    return pl.pallas_call(
        total_kernel,
        out_shape=(jax.ShapeDtypeStruct((rows, wide // 2), f32),) * 2,
        in_specs=[VM],
        out_specs=(VM,) * 2,
        compiler_params=PARAMS,
        cost_estimate=cost(1),
        name="total",
    )(terms)


def lay_kernel(*refs):
    out0, out1 = refs[-2:]
    for axis, parts, out in (("z", refs[:4], out0), ("x", refs[4:8], out1)):
        step = parts[0].shape[0]
        for n, ref in enumerate(parts):
            at = lax.rem(lax.axis_index(axis) + n, 4) * step
            out[pl.ds(pl.multiple_of(at, step), step), :] = ref[...]


def lay(left, right):
    rows, wide = left[0].shape
    return pl.pallas_call(
        lay_kernel,
        out_shape=(jax.ShapeDtypeStruct((4 * rows, wide), f32),) * 2,
        in_specs=[VM] * 8,
        out_specs=(VM,) * 2,
        compiler_params=PARAMS,
        cost_estimate=cost(1),
        name="lay",
    )(*left, *right)


def update_kernel(l0, l1, l2, l3, r0, r1, r2, r3, *refs):
    w_ref, w_acc_ref, hot_ref, hot_acc_ref, nw_ref, nwa_ref, nh_ref, nha_ref, grad_ref = refs
    part = w_ref.shape[1]
    step, half = l0.shape
    piece = step // 4
    i = pl.program_id(0)
    for d, left in enumerate((l0, l1, l2, l3)):

        @pl.when(lax.rem(lax.axis_index("x") + d, 4) == i)
        def _():
            grad_ref[:, :half] = left[...]

    start = pl.multiple_of(i * piece, piece)
    for d, right in enumerate((r0, r1, r2, r3)):
        at = lax.rem(lax.axis_index("z") + d, 4) * piece
        grad_ref[pl.ds(pl.multiple_of(at, piece), piece), half:] = right[pl.ds(start, piece), :]
    nw, nwa = adagrad(w_ref[...], w_acc_ref[...], grad_ref[:, :part])
    nw_ref[...] = nw
    nwa_ref[...] = nwa
    nh, nha = adagrad(hot_ref[...], hot_acc_ref[...], grad_ref[:, part:])
    nh_ref[...] = nh
    nha_ref[...] = nha


def update(left, right, w, w_acc, hot, hot_acc):
    step, half = left[0].shape
    w_block = pl.BlockSpec((step, w.shape[1]), lambda i: (i, 0))
    hot_block = pl.BlockSpec((step, hot.shape[1]), lambda i: (i, 0))
    return pl.pallas_call(
        update_kernel,
        grid=(4,),
        in_specs=[VM] * 8
        + [w_block] * 2
        + [hot_block] * 2,
        out_specs=(w_block, w_block, hot_block, hot_block),
        out_shape=(jax.ShapeDtypeStruct(w.shape, f32),) * 2
        + (jax.ShapeDtypeStruct(hot.shape, f32),) * 2,
        scratch_shapes=[pltpu.VMEM((step, 2 * half), f32)],
        compiler_params=PARAMS,
        cost_estimate=cost(4),
        name="update",
    )(*left, *right, w, w_acc, hot, hot_acc)


def stage_kernel(*refs):
    count = len(refs) // 2
    sems = refs[-1]
    copies = [
        pltpu.make_async_copy(refs[n], refs[count + n], sems.at[n]) for n in range(count)
    ]
    for copy in copies:
        copy.start()
    for copy in copies:
        copy.wait()


def stage(values):
    return pl.pallas_call(
        stage_kernel,
        out_shape=tuple(jax.ShapeDtypeStruct(value.shape, value.dtype) for value in values),
        in_specs=[HBM] * len(values),
        out_specs=(VM,) * len(values),
        scratch_shapes=[pltpu.SemaphoreType.DMA((len(values),))],
        compiler_params=PARAMS,
        cost_estimate=cost(4),
        name="stage",
    )(*values)


def cold_kernel(asked_ref, grads_ref, table_ref, acc_ref, new_ref, new_acc_ref):
    step, width = table_ref.shape
    slots = grads_ref.shape[0]
    rows = iota((step, slots), 0) + pl.program_id(0) * step
    onehot = jnp.where(asked_ref[...] == rows, 1.0, 0.0).astype(bf16)
    grad = jnp.dot(onehot, grads_ref[...], preferred_element_type=f32)
    param, acc = adagrad(table_ref[...], acc_ref[...], grad)
    new_ref[...] = param
    new_acc_ref[...] = acc


def cold_update(asked, grads, table, acc):
    rows, width = table.shape
    slots = grads.shape[0]
    step = 256
    block = pl.BlockSpec((step, width), lambda i: (i, 0))
    return pl.pallas_call(
        cold_kernel,
        grid=(rows // step,),
        out_shape=(jax.ShapeDtypeStruct(table.shape, f32),) * 2,
        in_specs=[
            pl.BlockSpec((1, slots), lambda i: (0, 0)),
            pl.BlockSpec((slots, width), lambda i: (0, 0)),
            block,
            block,
        ],
        out_specs=(block, block),
        compiler_params=PARAMS,
        cost_estimate=cost(5),
        name="cold_update",
    )(asked, grads, table, acc)


def along(value, axis, by):
    return lax.ppermute(value, axis, [((i + by) % 4, i) for i in range(4)])


def around(value, axis):
    last, one = along(value, axis, 3), along(value, axis, 1)
    return value, one, along(value, axis, 2), last


def swap(value):
    return lax.ppermute(value, "core", [(0, 1), (1, 0)])


def on_device(
    hot_ids,
    cold_owner,
    cold_row,
    cold_exp,
    labels,
    head_w,
    hot_table,
    hot_acc,
    cold_table,
    cold_acc,
    tower_w,
    tower_acc,
):
    devices = math.prod(lax.axis_size(name) for name in ALL)
    y, core = lax.axis_index("y"), lax.axis_index("core")
    me = 2 * y + core
    batch, keys = hot_ids.shape
    hot_rows, width = hot_table.shape
    part = tower_w.shape[1]
    capacity = max(2, 2 * batch * cold_owner.shape[1] // devices)
    asks, place, scale, half, quarter = route(
        cold_owner.T, cold_row.T, cold_exp.T, hot_table, tower_w, devices, capacity
    )
    asked = lax.all_to_all(asks, ALL, split_axis=0, concat_axis=0, tiled=True)
    spread_mat = spread(place, scale, capacity)
    quarters = tuple(along(quarter, "y", by) for by in (1, 2, 3))
    counts = count_of(hot_ids, hot_rows)
    cold_half = cold_table.astype(bf16)
    asked, counts, cold_half = lax.optimization_barrier((asked, counts, cold_half))
    count = quarter.shape[0] // 2
    by_x = jnp.stack([value[:count] for value in quarters])
    by_z = jnp.stack([value[count:] for value in quarters])
    looked = lookup(asked, cold_half)
    xs = tuple(along(by_x, "x", by) for by in (1, 2, 3))
    zs = tuple(along(by_z, "z", by) for by in (1, 2, 3))
    returned = lax.all_to_all(
        looked.reshape(devices, capacity, width), ALL, split_axis=0, concat_axis=0, tiled=True
    ).reshape(-1, width)
    pieces = lax.optimization_barrier((half, by_x) + xs + (by_z,) + zs)
    pieces += tuple(swap(value) for value in pieces)
    hot_feat = hot_pooled(counts, pieces, width)
    heads = head_w.reshape(4, 2, part)
    turned = jnp.concatenate([heads, heads])
    turned = lax.dynamic_slice_in_dim(turned, y, 4, 0)
    head = jnp.concatenate(
        [lax.dynamic_slice_in_dim(turned, side, 1, 1).reshape(1, -1) for side in (core, 1 - core)],
        axis=1,
    )
    outgoing, load = tower(
        hot_feat, returned, spread_mat, head, labels[:, None], hot_ids, pieces
    )
    loads = around(load, "y")
    outgoing, loads = lax.optimization_barrier((outgoing, loads))
    incoming = lax.all_to_all(
        outgoing.reshape(devices, capacity, width), ALL, split_axis=0, concat_axis=0, tiled=True
    ).reshape(-1, width)
    loads += tuple(swap(part) for part in loads)
    head_part = lax.dynamic_slice(head_w, (me * part,), (part,))[None, :]
    own, one, two, last = loads[:4]
    early = columns((own, loads[4], one, last), half, head_part, keys)
    partial = columns((two,) + loads[5:], half, head_part, keys, (early,))
    partial, incoming = lax.optimization_barrier((partial, incoming))
    terms = lax.all_to_all(partial, ("x", "z"), split_axis=0, concat_axis=0, tiled=True)
    new_cold = cold_update(asked.reshape(1, -1), incoming, cold_table, cold_acc)
    terms, (new_cold, new_cold_acc) = lax.optimization_barrier((terms, new_cold))
    left, right = total_of(terms.reshape(16, -1, part + width))
    left, right = lay(around(left, "z"), around(right, "x"))
    params = (tower_w, tower_acc, hot_table, hot_acc)
    left, right, params = lax.optimization_barrier((left, right, params))
    params = stage(params)
    left, right = around(left, "x"), around(right, "z")
    new_w, new_w_acc, new_hot, new_hot_acc = update(
        left, right, *params
    )
    return (new_hot, new_hot_acc, new_cold, new_cold_acc, new_w, new_w_acc)


def solution(mesh):
    chips = mesh.devices.reshape(4, 2, 4, 4)
    mesh = jax.sharding.Mesh(chips, ALL)
    split = P(ALL, None)
    rows = P(TABLE, None)
    cols = P(None, TABLE)
    return jax.shard_map(
        on_device,
        mesh=mesh,
        in_specs=(split,) * 4 + (P(ALL), P(), rows, rows, split, split, cols, cols),
        out_specs=(rows, rows, split, split, cols, cols),
        check_vma=False,
    )
```
